512 devices in a mesh: dp: 16 (over y_hi, z), clip: 32 (over y_lo, x, core).
Axes of the slice: x: 4, y: 8 (y_hi: 2, y_lo: 4; y = y_hi * 4 + y_lo), z: 8, core: 2. Of those that a mesh axis runs over, the one named last changes fastest.
Arguments:
- clip_embed: bfloat16 [4096, 16, 1408], P(('dp', 'clip')), may hold values from -8 to 8
- clip_counts: int32 [4096], P(('dp', 'clip')), may hold values from 1 to 16
- pool_query: bfloat16 [1408], replicated, as said below
- proj_weight: bfloat16 [1408, 768], P('clip'), may hold values from -0.3 to 0.3
- text_embed: bfloat16 [4096, 768], P(('dp', 'clip')), may hold values from -8 to 8
- pair_index: int32 [4096], replicated, may hold values from 0 to 4095, each once
- logit_scale: float32 [1], replicated, may hold values from 10 to 40
Outputs:
- d_clips: bfloat16 [4096, 16, 1408], P(('dp', 'clip'))
- d_weight: float32 [1408, 768], P('clip')
- d_texts: float32 [4096, 768], P(('dp', 'clip'))
The draws below stay inside these ranges and needn't reach their ends.
Inputs may be any that keep to these rules, and one draw needn't show every extreme that they name: `pool_query`: independent normal values with standard deviation 2 / sqrt(1408).
All inputs are finite; a program needn't handle non-finite values.
Results may differ from the reference program's by a relative error of at most 0.022.
Values may be sent and summed in bfloat16 or wider, within the bound.
No kernel may reach another device: no remote copies, remote signals or barrier semaphores. Data moves between devices by JAX's collectives and lax.ppermute only.
A program may use at most 64 MiB of HBM per device.

```python
import math
import jax
import jax.numpy as jnp
from jax import lax

E = 1408
P_SIZE = 768
VID_LOC = 8
CLIPS = 16
VIDEOS = 4096
N_CLIP = 32


def common_query(key):
    return 2.0 * E ** (-0.5) * jax.random.normal(key, (E,), jnp.float32)


def common_direction(key):
    side_key = jax.random.fold_in(key, 91)
    flips = jax.random.bernoulli(side_key, 0.5, (P_SIZE,)).astype(jnp.float32)
    return (2.0 * flips - 1.0) * P_SIZE ** (-0.5)


def draw_pool_query(key, part):
    return common_query(key).astype(jnp.bfloat16)


def draw_proj_weight(key, part):
    direction = common_query(key)
    target = common_direction(key)
    key = jax.random.fold_in(key, 5)
    noise = jax.random.normal(key, (E, P_SIZE), jnp.float32) * E ** (-0.5)
    return jnp.clip(noise + 3.0 * direction[:, None] * target[None, :], -0.296875, 0.296875).astype(jnp.bfloat16)


def draw_text_embed(key, part):
    target = common_direction(key)
    key = jax.random.fold_in(key, 7)
    noise_key = jax.random.fold_in(key, 0)
    ramp = jnp.arange(VIDEOS, dtype=jnp.float32) / VIDEOS
    noise = jax.random.normal(noise_key, (VIDEOS, P_SIZE), jnp.float32)
    strength = 0.8
    text = noise + strength * ramp[:, None] * P_SIZE ** 0.5 * target[None, :]
    return jnp.clip(text, -8.0, 8.0).astype(jnp.bfloat16)


def draw_clip_embed(key, part):
    direction = common_query(key)
    key = jax.random.fold_in(key, 2)
    noise_key = jax.random.fold_in(key, 0)
    ramp = 3.0 * jnp.arange(VIDEOS, dtype=jnp.float32) / VIDEOS
    shift = ramp[:, None, None] * direction[None, None, :]
    base = jnp.clip(jax.random.normal(noise_key, (VIDEOS, CLIPS, E), jnp.float32), -6.0, 6.0)
    return jnp.clip(base + shift, -8.0, 8.0).astype(jnp.bfloat16)


def touch_ends(array, rng, smallest, high):
    longest = array.shape.index(max(array.shape))
    spots = []
    for shift in (0, 1):
        where = [jax.random.randint(jax.random.fold_in(rng, axis), (), 0, length) for axis, length in enumerate(array.shape)]
        where[longest] = (where[longest] + shift) % array.shape[longest]
        spots.append(tuple(where))
    return array.at[spots[0]].set(smallest).at[spots[1]].set(high)


def setup_inputs(seed: int = 0) -> dict:
    arg_keys = jax.random.split(jax.random.key(seed), 8)
    clip_embed = draw_clip_embed(jax.random.fold_in(arg_keys[7], 71), 0)
    clip_counts = touch_ends(jax.random.randint(arg_keys[1], (VIDEOS,), 1, CLIPS + 1), jax.random.fold_in(arg_keys[1], 1), 1, CLIPS).astype(jnp.int32)
    pool_query = draw_pool_query(jax.random.fold_in(arg_keys[7], 71), 0)
    proj_weight = draw_proj_weight(jax.random.fold_in(arg_keys[7], 71), 0)
    text_embed = draw_text_embed(jax.random.fold_in(arg_keys[7], 71), 0)
    pair_index = jax.random.permutation(arg_keys[5], VIDEOS).astype(jnp.int32)
    logit_scale = jnp.clip(jnp.exp(jax.random.uniform(arg_keys[6], (1,), jnp.float32, math.log(10.0), math.log(40.0))), 10.0, 40.0)
    return dict(clip_embed=clip_embed, clip_counts=clip_counts, pool_query=pool_query, proj_weight=proj_weight, text_embed=text_embed, pair_index=pair_index, logit_scale=logit_scale)


EPS = 1e-06

def unit_rows(values):
    norm_value = jnp.sqrt(lax.optimization_barrier(jnp.sum(values * values, axis=1, keepdims=True)) + EPS)
    return (values / norm_value, norm_value)

def reference(clip_embed, clip_counts, pool_query, proj_weight, text_embed, pair_index, logit_scale):
    query_f = pool_query.astype(jnp.float32)
    blocks = VIDEOS // VID_LOC
    clip_blocks = clip_embed.reshape(blocks, VID_LOC, CLIPS, E)
    count_blocks = clip_counts.reshape(blocks, VID_LOC)

    def pool_block(packed):
        embedding, counts_here = packed
        embedding_f = embedding.astype(jnp.float32)
        scores = jnp.einsum('vce,e->vc', embedding_f, query_f)
        position = jnp.arange(CLIPS, dtype=jnp.int32)
        usable = position[None, :] < counts_here[:, None]
        masked = jnp.where(usable, scores, -1e+30)
        top_score = lax.optimization_barrier(jnp.max(masked, axis=1, keepdims=True))
        raised = jnp.where(usable, jnp.exp(masked - top_score), 0.0)
        weights = raised / lax.optimization_barrier(jnp.sum(raised, axis=1, keepdims=True))
        summary = jnp.einsum('vc,vce->ve', weights, embedding_f)
        return (weights, summary)
    weights, summary = lax.map(pool_block, (clip_blocks, count_blocks))
    summary = summary.reshape(VIDEOS, E)
    summary_b = summary.astype(jnp.bfloat16)
    projected = jnp.dot(summary_b, proj_weight, preferred_element_type=jnp.float32)
    unit_video, video_norm = unit_rows(projected)
    unit_text, text_norm = unit_rows(text_embed.astype(jnp.float32))
    video_b = unit_video.astype(jnp.bfloat16)
    text_b = unit_text.astype(jnp.bfloat16)
    logit_mult = logit_scale[0]
    row_block = VID_LOC * N_CLIP
    groups = VIDEOS // row_block
    video_groups = video_b.reshape(groups, row_block, P_SIZE)

    def totals(rows_b):
        expo = jnp.exp(logit_mult * jnp.dot(rows_b, text_b.T, preferred_element_type=jnp.float32))
        return (lax.optimization_barrier(jnp.sum(expo, axis=1)), lax.optimization_barrier(jnp.sum(expo, axis=0)))
    row_total, col_parts = lax.map(totals, video_groups)
    col_total = lax.optimization_barrier(jnp.sum(col_parts, axis=0))
    every_index = jnp.arange(VIDEOS, dtype=jnp.int32)

    def grad_step(carry, packed):
        rows_b, row_here, pairs_here = packed
        expo = jnp.exp(logit_mult * jnp.dot(rows_b, text_b.T, preferred_element_type=jnp.float32))
        positive = (every_index[None, :] == pairs_here[:, None]).astype(jnp.float32)
        grad_logits = ((expo / row_here[:, None] + expo / col_total[None, :]) * 0.5 - positive).astype(jnp.bfloat16)
        video_part = logit_mult * jnp.dot(grad_logits, text_b, preferred_element_type=jnp.float32)
        carry = carry + logit_mult * jnp.dot(grad_logits.T, rows_b, preferred_element_type=jnp.float32)
        return (carry, video_part)
    d_text, d_video = lax.scan(grad_step, jnp.zeros((VIDEOS, P_SIZE), jnp.float32), (video_groups, row_total, pair_index.reshape(groups, row_block)))
    d_video = d_video.reshape(VIDEOS, P_SIZE)
    d_projected = ((d_video - unit_video * lax.optimization_barrier(jnp.sum(unit_video * d_video, axis=1, keepdims=True))) / video_norm).astype(jnp.bfloat16)
    d_texts = (d_text - unit_text * lax.optimization_barrier(jnp.sum(unit_text * d_text, axis=1, keepdims=True))) / text_norm
    d_weight = jnp.dot(summary_b.T, d_projected, preferred_element_type=jnp.float32)
    d_summary = jnp.dot(d_projected, proj_weight.T, preferred_element_type=jnp.float32)

    def clip_block(packed):
        embedding, weights_here, summary_here, grad_here = packed
        embedding_f = embedding.astype(jnp.float32)
        aligned = jnp.einsum('vce,ve->vc', embedding_f, grad_here)
        baseline = lax.optimization_barrier(jnp.sum(grad_here * summary_here, axis=1, keepdims=True))
        d_scores = weights_here * (aligned - baseline)
        result = weights_here[:, :, None] * grad_here[:, None, :] + d_scores[:, :, None] * query_f[None, None, :]
        return result.astype(jnp.bfloat16)
    d_clips = lax.map(clip_block, (clip_blocks, weights, summary.reshape(blocks, VID_LOC, E), d_summary.reshape(blocks, VID_LOC, E)))
    return (d_clips.reshape(VIDEOS, CLIPS, E), d_weight, d_texts)
```

```python
import jax
import jax.numpy as jnp
from jax import lax
from jax.sharding import Mesh, PartitionSpec as P

EPS = 1e-06
F32 = jnp.float32
BF16 = jnp.bfloat16
DP = ("yh", "z")
CLIP = ("yl", "x", "core")
NEAR = ("x", "core")


def unit_rows(values):
    norm_value = jnp.sqrt(jnp.sum(values * values, axis=1, keepdims=True) + EPS)
    return (values / norm_value, norm_value)


def exchange(blocks, axes):
    return lax.all_to_all(blocks, axes, split_axis=0, concat_axis=0, tiled=True)


def gather(block, axes):
    return exchange(jnp.broadcast_to(block[None], (lax.axis_size(axes), *block.shape)), axes)


def shards(clip_embed, clip_counts, pool_query, proj_weight, text_embed, pair_index, logit_scale):
    n_loc, n_clips, width = clip_embed.shape
    joint = proj_weight.shape[1]
    w_rows = proj_weight.shape[0]
    n_dp = lax.axis_size(DP)
    group_id = lax.axis_index(DP)
    lane_id = lax.axis_index(CLIP)
    yl_id = lax.axis_index("yl")
    near_id = lax.axis_index(NEAR)
    core_id = lax.axis_index("core")
    scale = logit_scale[0]

    unit_text, text_norm = unit_rows(text_embed.astype(F32))
    text_b = unit_text.astype(BF16)
    lane_texts = gather(text_b, DP).reshape(n_dp * n_loc, joint)

    query_f = pool_query.astype(F32)
    embed_f = clip_embed.astype(F32)
    scores = jnp.einsum("vce,e->vc", embed_f, query_f)
    usable = jnp.arange(n_clips, dtype=jnp.int32)[None, :] < clip_counts[:, None]
    masked = jnp.where(usable, scores, -1e30)
    raised = jnp.where(usable, jnp.exp(masked - jnp.max(masked, axis=1, keepdims=True)), 0.0)
    weights = raised / jnp.sum(raised, axis=1, keepdims=True)
    summary = jnp.einsum("vc,vce->ve", weights, embed_f)
    summary_b = summary.astype(BF16)

    w_pad = -(-w_rows // 16) * 16
    payload = jnp.concatenate(
        [
            lane_texts,
            jnp.pad(proj_weight, ((0, w_pad - w_rows), (0, 0))),
            summary_b[:, :joint],
            jnp.pad(summary_b[:, joint:], ((0, 0), (0, 2 * joint - width))),
        ],
        axis=0,
    )
    n_lane = lane_texts.shape[0]
    over_y = gather(payload, "yl")
    texts = over_y[:, :n_lane].reshape(-1, joint)
    over_x = gather(over_y[:, n_lane:], "x")
    other = lax.ppermute(over_x, "core", [(0, 1), (1, 0)])
    both = jnp.where(
        core_id == 0, jnp.stack([over_x, other], axis=1), jnp.stack([other, over_x], axis=1)
    )
    full_weight = both[..., :w_rows, :].transpose(2, 0, 1, 3, 4).reshape(width, joint)
    low = both[..., w_pad : w_pad + n_loc, :]
    high = both[..., w_pad + n_loc :, : width - joint]
    summaries = jnp.concatenate([low, high], axis=-1).reshape(-1, width)

    projected = jnp.dot(summaries, full_weight, preferred_element_type=F32)
    unit_video, video_norm = unit_rows(projected)
    video_b = unit_video.astype(BF16)
    expo = jnp.exp(
        scale * lax.dot_general(video_b, texts, (((1,), (1,)), ((), ())), preferred_element_type=F32)
    )
    row_part = jnp.sum(expo, axis=1)
    col_part = jnp.sum(expo, axis=0)
    row_total = jnp.sum(gather(row_part[None], NEAR), axis=(0, 1))
    col_total = jnp.sum(gather(col_part[None], DP), axis=(0, 1))

    n_yl = lax.axis_size("yl")
    n_x = lax.axis_size("x")
    group_rows = n_loc * n_yl * n_x * 2
    pairs = lax.dynamic_slice(pair_index, (group_id * group_rows,), (group_rows,))
    pairs = pairs.reshape(n_yl, n_x * 2, n_loc).transpose(1, 0, 2).reshape(-1)
    col_id = (
        (
            jnp.arange(n_dp, dtype=jnp.int32)[None, :, None] * (n_yl * n_x * 2)
            + jnp.arange(n_yl, dtype=jnp.int32)[:, None, None] * (n_x * 2)
            + near_id
        )
        * n_loc
        + jnp.arange(n_loc, dtype=jnp.int32)[None, None, :]
    ).reshape(-1)
    positive = (col_id[None, :] == pairs[:, None]).astype(F32)
    grad_logits = ((expo / row_total[:, None] + expo / col_total[None, :]) * 0.5 - positive).astype(BF16)

    video_part = scale * jnp.dot(grad_logits, texts, preferred_element_type=F32)
    n_near = lax.axis_size(NEAR)
    near_rows = group_rows // n_near
    received = exchange(video_part.astype(BF16).reshape(n_near, near_rows, joint), NEAR)
    d_video = jnp.sum(received.astype(F32), axis=0)
    unit_near = lax.dynamic_slice(unit_video, (near_id * near_rows, 0), (near_rows, joint))
    norm_near = lax.dynamic_slice(video_norm, (near_id * near_rows, 0), (near_rows, 1))
    d_near = (
        (d_video - unit_near * jnp.sum(unit_near * d_video, axis=1, keepdims=True)) / norm_near
    ).astype(BF16)
    d_projected = gather(d_near, NEAR).reshape(group_rows, joint)

    own_cols = lax.dynamic_slice(grad_logits, (0, yl_id * n_lane), (group_rows, n_lane))
    text_part = scale * lax.dot_general(
        own_cols, video_b, (((0,), (0,)), ((), ())), preferred_element_type=F32
    )
    summary_cols = lax.dynamic_slice(summaries, (0, lane_id * w_rows), (group_rows, w_rows))
    weight_part = lax.dot_general(
        summary_cols, d_projected, (((0,), (0,)), ((), ())), preferred_element_type=F32
    )
    piece = -(-w_rows // n_dp)
    weight_part = jnp.pad(weight_part, ((0, piece * n_dp - w_rows), (0, 0)))
    sums = exchange(
        jnp.concatenate(
            [
                text_part.astype(BF16).reshape(n_dp, n_loc, joint),
                weight_part.astype(BF16).reshape(n_dp, piece, joint),
            ],
            axis=1,
        ),
        DP,
    )
    sums = jnp.sum(sums.astype(F32), axis=0)
    d_text = sums[:n_loc]
    d_texts = (d_text - unit_text * jnp.sum(unit_text * d_text, axis=1, keepdims=True)) / text_norm
    d_weight = gather(sums[n_loc:], DP).reshape(piece * n_dp, joint)[:w_rows]

    d_own = lax.dynamic_slice(d_near, (yl_id * n_loc, 0), (n_loc, joint))
    d_summary = lax.dot_general(
        d_own, full_weight, (((1,), (1,)), ((), ())), preferred_element_type=F32
    )
    aligned = jnp.einsum("vce,ve->vc", embed_f, d_summary)
    baseline = jnp.sum(d_summary * summary, axis=1, keepdims=True)
    d_scores = weights * (aligned - baseline)
    d_clips = (
        weights[:, :, None] * d_summary[:, None, :] + d_scores[:, :, None] * query_f[None, None, :]
    ).astype(BF16)
    return (d_clips, d_weight, d_texts)


def solution(mesh):
    fine = Mesh(mesh.devices.reshape(2, 8, 4, 4, 2), DP + CLIP)
    everywhere = DP + CLIP
    return jax.shard_map(
        shards,
        mesh=fine,
        in_specs=(
            P(everywhere, None, None),
            P(everywhere),
            P(),
            P(CLIP, None),
            P(everywhere, None),
            P(),
            P(),
        ),
        out_specs=(P(everywhere, None, None), P(CLIP, None), P(everywhere, None)),
        check_vma=False,
    )
```

```python
import functools

import jax
import jax.numpy as jnp
from jax import lax
from jax.experimental import pallas as pl
from jax.experimental.pallas import tpu as pltpu
from jax.sharding import Mesh, PartitionSpec as P

EPS = 1e-06
F32 = jnp.float32
BF16 = jnp.bfloat16
DP = ("yh", "z")
CLIP = ("yl", "x", "core")
PLANE = ("yl", "x")
SWAP = [(0, 1), (1, 0)]


def unit_rows(values):
    norm_value = jnp.sqrt(jnp.sum(values * values, axis=1, keepdims=True) + EPS)
    return (values / norm_value, norm_value)


def exchange(blocks, axes):
    return lax.all_to_all(blocks, axes, split_axis=0, concat_axis=0, tiled=True)


def dot(a, b, contract):
    return lax.dot_general(a, b, (contract, ((), ())), preferred_element_type=F32)


def local(body, outs, n_scalars, n_args, scratch=(), flops=1e6, moved=1e6):
    vmem = pl.BlockSpec(memory_space=pltpu.VMEM)
    smem = pl.BlockSpec(memory_space=pltpu.SMEM)
    return pl.pallas_call(
        body,
        out_shape=tuple(jax.ShapeDtypeStruct(shape, dtype) for shape, dtype in outs),
        in_specs=[smem] * n_scalars + [vmem] * n_args,
        out_specs=tuple(vmem for _ in outs),
        scratch_shapes=list(scratch),
        compiler_params=pltpu.CompilerParams(vmem_limit_bytes=40 * 1024 * 1024),
        cost_estimate=pl.CostEstimate(flops=int(flops), bytes_accessed=int(moved), transcendentals=0),
    )


def text_body(text_ref, out_ref):
    unit, _ = unit_rows(text_ref[...].astype(F32))
    out_ref[...] = jnp.broadcast_to(unit[None], out_ref.shape).astype(BF16)


def column(row):
    return jnp.broadcast_to(row, (128, row.shape[1])).T[:, :1]


def logits_body(
    n_loc, w_rows, pos_ref, scale_ref, own_ref, other_ref, text_own_ref, text_other_ref,
    weight_ref, summary_ref, video_ref, unit_ref, norm_ref, expo_ref, rows_ref, cols_ref,
    weight_f, summary_f, unit_f, norm_f,
):
    n_x, n_yl, _, joint = own_ref.shape
    width = weight_ref.shape[0]
    half = n_x * n_yl * n_loc
    w_pad = -(-w_rows // 16) * 16
    first = pos_ref[0] == 0
    for x in range(n_x):
        for yl in range(n_yl):
            own = own_ref[x, yl].astype(F32)
            other = other_ref[x, yl].astype(F32)
            pair = (jnp.where(first, own, other), jnp.where(first, other, own))
            for core in range(2):
                at = ((yl * n_x + x) * 2 + core) * w_rows
                weight_f[at : at + w_rows, :] = pair[core][:w_rows]
                row = core * half + (yl * n_x + x) * n_loc
                summary_f[row : row + n_loc, :joint] = pair[core][w_pad : w_pad + n_loc]
                summary_f[row : row + n_loc, joint:] = pair[core][w_pad + n_loc :, : width - joint]
    weight_b = weight_f[...].astype(BF16)
    summary_b = summary_f[...].astype(BF16)
    weight_ref[...] = weight_b
    summary_ref[...] = summary_b
    unit, norm = unit_rows(dot(summary_b, weight_b, ((1,), (0,))))
    video_b = unit.astype(BF16)
    video_ref[...] = video_b
    unit_f[...] = unit
    norm_f[...] = jnp.broadcast_to(norm, norm_f.shape)
    mine = pl.ds(pl.multiple_of(pos_ref[1] * n_loc, n_loc), n_loc)
    unit_ref[...] = unit_f[mine, :]
    norm_ref[...] = norm_f[mine, :]
    n_lane = text_own_ref.shape[0]
    scale = scale_ref[0]
    expo_ref[:, :n_lane] = jnp.exp(scale * dot(video_b, text_own_ref[...], ((1,), (1,))))
    expo_ref[:, n_lane:] = jnp.exp(scale * dot(video_b, text_other_ref[...], ((1,), (1,))))
    expo = expo_ref[...]
    row_part = jnp.broadcast_to(jnp.sum(expo, axis=1, keepdims=True), (2 * half, 128)).T[:1]
    col_part = jnp.sum(expo, axis=0, keepdims=True)
    rows_ref[...] = jnp.broadcast_to(row_part[None], rows_ref.shape)
    cols_ref[...] = jnp.broadcast_to(col_part[None], cols_ref.shape)


def grad_body(
    n_loc, n_clip, pos_ref, scale_ref, expo_ref, rows_ref, cols_ref, pairs_ref, text_own_ref,
    text_other_ref, grad_ref, part_ref,
):
    n_lane = text_own_ref.shape[0]
    rows = jnp.sum(rows_ref[...], axis=0)
    cols = jnp.sum(cols_ref[...], axis=0)
    core = pos_ref[0]
    at = lax.broadcasted_iota(jnp.int32, (1, 2 * n_lane), 1)
    lane = jnp.where(at < n_lane, pos_ref[2], pos_ref[3])
    slot = jnp.where(at < n_lane, at, at - n_lane)
    col_id = ((slot // n_loc) * n_clip + lane) * n_loc + slot % n_loc
    positive = jnp.where(pairs_ref[...] == col_id, 1.0, 0.0)
    expo = expo_ref[...]
    grad = (expo / column(rows) + expo / cols) * 0.5 - positive
    grad_ref[...] = grad.astype(BF16)
    half = expo.shape[0] // 2
    mine = grad_ref[pl.ds(pl.multiple_of(core * half, half), half), :]
    part = dot(mine[:, :n_lane], text_own_ref[...], ((1,), (0,)))
    part = part + dot(mine[:, n_lane:], text_other_ref[...], ((1,), (0,)))
    part_ref[...] = (scale_ref[0] * part).astype(BF16)


def text_part_body(scale_ref, grad_ref, video_ref, out_ref):
    n_lane = out_ref.shape[0]
    part = dot(grad_ref[:, :n_lane], video_ref[...], ((0,), (0,)))
    out_ref[...] = (scale_ref[0] * part).astype(BF16)


def projected_body(part_ref, unit_ref, norm_ref, out_ref, own_ref):
    d_video = jnp.sum(part_ref[...].astype(F32), axis=0)
    unit = unit_ref[...]
    norm = norm_ref[:, :1]
    value = (d_video - unit * jnp.sum(unit * d_video, axis=1, keepdims=True)) / norm
    out_ref[...] = jnp.broadcast_to(value[None], out_ref.shape).astype(BF16)
    own_ref[...] = value.astype(BF16)


def weight_body(pos_ref, cols_ref, own_ref, other_ref, text_ref, send_ref, part_ref):
    half = own_ref.shape[0]
    core = pos_ref[0]
    own_cols = cols_ref[pl.ds(pl.multiple_of(core * half, half), half), :]
    other_cols = cols_ref[pl.ds(pl.multiple_of((1 - core) * half, half), half), :]
    part = dot(own_cols, own_ref[...], ((0,), (0,))) + dot(other_cols, other_ref[...], ((0,), (0,)))
    part_ref[...] = part
    n_text = text_ref.shape[0] // 2
    away = (1 - pos_ref[4]) * n_text
    send_ref[:n_text, :] = text_ref[pl.ds(pl.multiple_of(away, n_text), n_text), :]
    send_ref[n_text:, :] = part.astype(BF16)


def near_sum_body(pos_ref, part_ref, text_ref, got_ref, out_ref):
    n_text = text_ref.shape[0] // 2
    here = pl.ds(pl.multiple_of(pos_ref[4] * n_text, n_text), n_text)
    got = got_ref[...].astype(F32)
    text = text_ref[here, :].astype(F32) + got[:n_text]
    weight = part_ref[...] + got[n_text:]
    n_z = out_ref.shape[0]
    n_loc = n_text // n_z
    for z in range(n_z):
        rows = jnp.concatenate([text[z * n_loc : (z + 1) * n_loc], weight], axis=0)
        out_ref[z] = rows.astype(BF16)


def last_body(got_ref, text_ref, d_weight_ref, d_texts_ref):
    total = jnp.sum(got_ref[...].astype(F32), axis=0)
    n_loc = text_ref.shape[0]
    unit, norm = unit_rows(text_ref[...].astype(F32))
    d_text = total[:n_loc]
    d_texts_ref[...] = (d_text - unit * jnp.sum(unit * d_text, axis=1, keepdims=True)) / norm
    d_weight_ref[...] = total[n_loc : n_loc + d_weight_ref.shape[0]]


def shards(clip_embed, clip_counts, pool_query, proj_weight, text_embed, pair_index, logit_scale):
    n_loc, n_clips, width = clip_embed.shape
    w_rows, joint = proj_weight.shape
    n_dp, n_yh, n_z = lax.axis_size(DP), lax.axis_size("yh"), lax.axis_size("z")
    n_yl, n_x, n_clip = lax.axis_size("yl"), lax.axis_size("x"), lax.axis_size(CLIP)
    n_plane = n_yl * n_x
    group_rows = n_loc * n_clip
    half = group_rows // 2
    n_lane = n_dp * n_loc
    core_id = lax.axis_index("core")
    plane_id = lax.axis_index(PLANE)
    lane_id = lax.axis_index(CLIP)
    group_id = lax.axis_index(DP)
    pos = jnp.stack(
        [
            core_id,
            core_id * n_plane + plane_id,
            lane_id,
            plane_id * 2 + (1 - core_id),
            lax.axis_index("yh"),
        ]
    ).astype(jnp.int32)

    (text_send,) = local(text_body, [((n_dp, n_loc, joint), BF16)], 0, 1)(text_embed)
    text_own = exchange(text_send, DP).reshape(n_lane, joint)
    text_other = lax.ppermute(text_own, "core", SWAP)

    query_f = pool_query.astype(F32)
    embed_f = clip_embed.astype(F32)
    scores = jnp.einsum("vce,e->vc", embed_f, query_f)
    usable = jnp.arange(n_clips, dtype=jnp.int32)[None, :] < clip_counts[:, None]
    masked = jnp.where(usable, scores, -1e30)
    raised = jnp.where(usable, jnp.exp(masked - jnp.max(masked, axis=1, keepdims=True)), 0.0)
    weights = raised / jnp.sum(raised, axis=1, keepdims=True)
    summary = jnp.einsum("vc,vce->ve", weights, embed_f)
    summary_b = summary.astype(BF16)

    w_pad = -(-w_rows // 16) * 16
    payload = jnp.concatenate(
        [
            jnp.pad(proj_weight, ((0, w_pad - w_rows), (0, 0))),
            summary_b[:, :joint],
            jnp.pad(summary_b[:, joint:], ((0, 0), (0, 2 * joint - width))),
        ],
        axis=0,
    )
    over_y = exchange(jnp.broadcast_to(payload[None], (n_yl, *payload.shape)), "yl")
    over_x = exchange(jnp.broadcast_to(over_y[None], (n_x, *over_y.shape)), "x")
    over_x_other = lax.ppermute(over_x, "core", SWAP)

    full_weight, summaries, video_b, unit_own, norm_own, expo, row_send, col_send = local(
        functools.partial(logits_body, n_loc, w_rows),
        [
            ((width, joint), BF16),
            ((group_rows, width), BF16),
            ((group_rows, joint), BF16),
            ((n_loc, joint), F32),
            ((n_loc, 128), F32),
            ((group_rows, 2 * n_lane), F32),
            ((n_plane, 1, group_rows), F32),
            ((n_dp, 1, 2 * n_lane), F32),
        ],
        2,
        4,
        scratch=[
            pltpu.VMEM((width, joint), F32),
            pltpu.VMEM((group_rows, width), F32),
            pltpu.VMEM((group_rows, joint), F32),
            pltpu.VMEM((group_rows, 128), F32),
        ],
        flops=7e8,
        moved=8e6,
    )(pos, logit_scale, over_x, over_x_other, text_own, text_other)
    rows = exchange(row_send, PLANE)
    cols = exchange(col_send, DP)

    pairs = lax.dynamic_slice(pair_index, (group_id * group_rows,), (group_rows,))
    pairs = pairs.reshape(n_plane, 2, n_loc).transpose(1, 0, 2).reshape(group_rows, 1)
    grad_logits, video_part = local(
        functools.partial(grad_body, n_loc, n_clip),
        [((group_rows, 2 * n_lane), BF16), ((half, joint), BF16)],
        2,
        6,
        flops=1e8,
    )(pos, logit_scale, expo, rows, cols, pairs, text_own, text_other)

    got_video = exchange(video_part.reshape(n_plane, n_loc, joint), PLANE)
    (text_part,) = local(text_part_body, [((n_lane, joint), BF16)], 1, 2, flops=1e8)(
        logit_scale, grad_logits, video_b
    )
    d_send, d_own = local(
        projected_body, [((n_plane, n_loc, joint), BF16), ((n_loc, joint), BF16)], 0, 3
    )(got_video, unit_own, norm_own)
    d_half = exchange(d_send, PLANE).reshape(half, joint)
    d_half_other = lax.ppermute(d_half, "core", SWAP)

    d_summary = dot(d_own, full_weight, ((1,), (1,)))
    aligned = jnp.einsum("vce,ve->vc", embed_f, d_summary)
    baseline = jnp.sum(d_summary * summary, axis=1, keepdims=True)
    d_scores = weights * (aligned - baseline)
    d_clips = (
        weights[:, :, None] * d_summary[:, None, :] + d_scores[:, :, None] * query_f[None, None, :]
    ).astype(BF16)

    summary_cols = lax.dynamic_slice(summaries, (0, lane_id * w_rows), (group_rows, w_rows))
    summary_cols = jnp.pad(summary_cols, ((0, 0), (0, w_pad - w_rows)))
    n_text = n_z * n_loc
    send, weight_part = local(
        weight_body, [((n_text + w_pad, joint), BF16), ((w_pad, joint), F32)], 1, 4, flops=3e7
    )(pos, summary_cols, d_half, d_half_other, text_part)
    got = lax.ppermute(send, "yh", SWAP)
    (sums,) = local(near_sum_body, [((n_z, n_loc + w_pad, joint), BF16)], 1, 3)(
        pos, weight_part, text_part, got
    )
    d_weight, d_texts = local(
        last_body, [((w_rows, joint), F32), ((n_loc, joint), F32)], 0, 2
    )(exchange(sums, "z"), text_embed)
    return (d_clips, d_weight, d_texts)


def solution(mesh):
    fine = Mesh(mesh.devices.reshape(2, 8, 4, 4, 2), DP + CLIP)
    everywhere = DP + CLIP
    return jax.shard_map(
        shards,
        mesh=fine,
        in_specs=(
            P(everywhere, None, None),
            P(everywhere),
            P(),
            P(CLIP, None),
            P(everywhere, None),
            P(),
            P(),
        ),
        out_specs=(P(everywhere, None, None), P(CLIP, None), P(everywhere, None)),
        check_vma=False,
    )
```

```python
import functools

import jax
import jax.numpy as jnp
from jax import lax
from jax.experimental import pallas as pl
from jax.experimental.pallas import tpu as pltpu
from jax.sharding import Mesh, PartitionSpec as P

EPS = 1e-06
F32 = jnp.float32
BF16 = jnp.bfloat16
DP = ("yh", "z")
CLIP = ("yl", "x", "core")
PLANE = ("yl", "x")
SWAP = [(0, 1), (1, 0)]


def unit_rows(values):
    norm_value = jnp.sqrt(jnp.sum(values * values, axis=1, keepdims=True) + EPS)
    return (values / norm_value, norm_value)


def exchange(blocks, axes):
    return lax.all_to_all(blocks, axes, split_axis=0, concat_axis=0, tiled=True)


def dot(a, b, contract):
    return lax.dot_general(a, b, (contract, ((), ())), preferred_element_type=F32)


def local(body, outs, n_scalars, n_args, n_far=0, scratch=(), flops=1e6, moved=1e6, mib=8):
    vmem = pl.BlockSpec(memory_space=pltpu.VMEM)
    smem = pl.BlockSpec(memory_space=pltpu.SMEM)
    far = pl.BlockSpec(memory_space=pltpu.HBM)
    return pl.pallas_call(
        body,
        out_shape=tuple(jax.ShapeDtypeStruct(shape, dtype) for shape, dtype in outs),
        in_specs=[smem] * n_scalars + [vmem] * n_args + [far] * n_far,
        out_specs=tuple(vmem for _ in outs),
        scratch_shapes=list(scratch),
        compiler_params=pltpu.CompilerParams(vmem_limit_bytes=mib * 1024 * 1024),
        cost_estimate=pl.CostEstimate(flops=int(flops), bytes_accessed=int(moved), transcendentals=0),
    )


def text_body(text_ref, out_ref):
    unit, _ = unit_rows(text_ref[...].astype(F32))
    out_ref[...] = jnp.broadcast_to(unit[None], out_ref.shape).astype(BF16)


def pool(counts_ref, embed, query):
    n_loc, n_clips, _ = embed.shape
    scores = jnp.sum(embed * query[None], axis=2, keepdims=True)
    video = lax.broadcasted_iota(jnp.int32, (n_loc, n_clips, 1), 0)
    clip = lax.broadcasted_iota(jnp.int32, (n_loc, n_clips, 1), 1)
    count = jnp.zeros((n_loc, n_clips, 1), jnp.int32)
    for v in range(n_loc):
        count = jnp.where(video == v, counts_ref[v], count)
    usable = clip < count
    masked = jnp.where(usable, scores, -1e30)
    raised = jnp.where(usable, jnp.exp(masked - jnp.max(masked, axis=1, keepdims=True)), 0.0)
    weights = raised / jnp.sum(raised, axis=1, keepdims=True)
    return weights, jnp.sum(weights * embed, axis=1)


def fetch(sources, targets, sems):
    copies = [
        pltpu.make_async_copy(source, target, sems.at[i])
        for i, (source, target) in enumerate(zip(sources, targets))
    ]
    for copy in copies:
        copy.start()
    for copy in copies:
        copy.wait()


def pool_body(
    query_ref, counts_hbm, clips_hbm, rows_hbm, payload_ref, counts_ref, clips_ref, rows_ref, sems
):
    fetch((counts_hbm, clips_hbm, rows_hbm), (counts_ref, clips_ref, rows_ref), sems)
    n_loc, _, width = clips_ref.shape
    w_rows, joint = rows_ref.shape
    w_pad = payload_ref.shape[0] - 2 * n_loc
    _, summary = pool(counts_ref, clips_ref[...].astype(F32), query_ref[...].astype(F32))
    high = jnp.concatenate(
        [summary[:, joint:], jnp.zeros((n_loc, 2 * joint - width), F32)], axis=1
    )
    tail = jnp.zeros((w_pad - w_rows, joint), F32)
    payload_ref[...] = jnp.concatenate(
        [rows_ref[...].astype(F32), tail, summary[:, :joint], high], axis=0
    ).astype(BF16)


def clips_body(
    d_own_ref, query_ref, counts_hbm, clips_hbm, weight_hbm, out_ref,
    counts_ref, clips_ref, weight_ref, sems,
):
    fetch((counts_hbm, clips_hbm, weight_hbm), (counts_ref, clips_ref, weight_ref), sems)
    embed = clips_ref[...].astype(F32)
    query = query_ref[...].astype(F32)
    weights, summary = pool(counts_ref, embed, query)
    d_summary = dot(d_own_ref[...], weight_ref[...], ((1,), (1,)))
    aligned = jnp.sum(embed * d_summary[:, None, :], axis=2, keepdims=True)
    baseline = jnp.sum(d_summary * summary, axis=1, keepdims=True)
    d_scores = weights * (aligned - baseline[:, None, :])
    out_ref[...] = (weights * d_summary[:, None, :] + d_scores * query[None]).astype(BF16)


def column(row):
    return jnp.broadcast_to(row, (128, row.shape[1])).T[:, :1]


def logits_body(
    n_loc, w_rows, scale_ref, own_ref, other_ref, text_own_ref, text_other_ref,
    _, weight_ref, summary_ref, video_ref, unit_ref, norm_ref, expo_ref, rows_ref, cols_ref,
    weight_f, summary_f, unit_f, norm_f,
):
    n_x, n_yl, _, joint = own_ref.shape
    width = weight_ref.shape[0]
    half = n_x * n_yl * n_loc
    w_pad = -(-w_rows // 16) * 16
    first = lax.axis_index("core") == 0
    yl_id = lax.axis_index("yl")
    for x in range(n_x):
        for yl in range(n_yl):
            slot = jnp.bitwise_xor(yl_id, yl)
            own = own_ref[x, slot].astype(F32)
            other = other_ref[x, slot].astype(F32)
            pair = (jnp.where(first, own, other), jnp.where(first, other, own))
            for core in range(2):
                at = ((yl * n_x + x) * 2 + core) * w_rows
                weight_f[at : at + w_rows, :] = pair[core][:w_rows]
                row = core * half + (yl * n_x + x) * n_loc
                summary_f[row : row + n_loc, :joint] = pair[core][w_pad : w_pad + n_loc]
                summary_f[row : row + n_loc, joint:] = pair[core][w_pad + n_loc :, : width - joint]
    weight_b = weight_f[...].astype(BF16)
    summary_b = summary_f[...].astype(BF16)
    weight_ref[...] = weight_b
    summary_ref[...] = summary_b
    unit, norm = unit_rows(dot(summary_b, weight_b, ((1,), (0,))))
    video_b = unit.astype(BF16)
    video_ref[...] = video_b
    unit_f[...] = unit
    norm_f[...] = jnp.broadcast_to(norm, norm_f.shape)
    place = (lax.axis_index("core") * n_yl + yl_id) * n_x + lax.axis_index("x")
    mine = pl.ds(pl.multiple_of(place * n_loc, n_loc), n_loc)
    unit_ref[...] = unit_f[mine, :]
    norm_ref[...] = norm_f[mine, :]
    n_lane = text_own_ref.shape[0]
    scale = scale_ref[0]
    expo_ref[:, :n_lane] = jnp.exp(scale * dot(video_b, text_own_ref[...], ((1,), (1,))))
    expo_ref[:, n_lane:] = jnp.exp(scale * dot(video_b, text_other_ref[...], ((1,), (1,))))
    expo = expo_ref[...]
    row_part = jnp.broadcast_to(jnp.sum(expo, axis=1, keepdims=True), (2 * half, 128)).T[:1]
    col_part = jnp.sum(expo, axis=0, keepdims=True)
    rows_ref[...] = jnp.broadcast_to(row_part[None], rows_ref.shape)
    cols_ref[...] = jnp.broadcast_to(col_part[None], cols_ref.shape)


def grad_body(
    n_loc, n_clip, scale_ref, expo_ref, rows_ref, cols_ref, pairs_ref, text_own_ref,
    text_other_ref, video_ref, part_ref, text_part_ref, grad_ref,
):
    n_lane = text_own_ref.shape[0]
    rows = jnp.sum(rows_ref[...], axis=0)
    cols = jnp.sum(cols_ref[...], axis=0)
    core = lax.axis_index("core")
    plane = lax.axis_index("yl") * lax.axis_size("x") + lax.axis_index("x")
    at = lax.broadcasted_iota(jnp.int32, (1, 2 * n_lane), 1)
    lane = jnp.where(at < n_lane, plane * 2 + core, plane * 2 + (1 - core))
    slot = jnp.where(at < n_lane, at, at - n_lane)
    col_id = ((slot // n_loc) * n_clip + lane) * n_loc + slot % n_loc
    group = lax.axis_index("yh") * lax.axis_size("z") + lax.axis_index("z")
    pairs = column(pairs_ref[pl.ds(group, 1), :].astype(F32)).astype(jnp.int32)
    pairs = pairs.reshape(-1, 2, n_loc, 1)
    pairs = jnp.concatenate([pairs[:, 0], pairs[:, 1]], axis=0).reshape(-1, 1)
    positive = jnp.where(pairs == col_id, 1.0, 0.0)
    expo = expo_ref[...]
    grad = (expo / column(rows) + expo / cols) * 0.5 - positive
    grad_ref[...] = grad.astype(BF16)
    half = expo.shape[0] // 2
    mine = grad_ref[pl.ds(pl.multiple_of(core * half, half), half), :]
    part = dot(mine[:, :n_lane], text_own_ref[...], ((1,), (0,)))
    part = part + dot(mine[:, n_lane:], text_other_ref[...], ((1,), (0,)))
    part_ref[...] = (scale_ref[0] * part).astype(BF16)
    text_part = dot(grad_ref[:, :n_lane], video_ref[...], ((0,), (0,)))
    text_part_ref[...] = (scale_ref[0] * text_part).astype(BF16)


def projected_body(part_ref, unit_ref, norm_ref, out_ref, own_ref):
    d_video = jnp.sum(part_ref[...].astype(F32), axis=0)
    unit = unit_ref[...]
    norm = norm_ref[:, :1]
    value = (d_video - unit * jnp.sum(unit * d_video, axis=1, keepdims=True)) / norm
    out_ref[...] = jnp.broadcast_to(value[None], out_ref.shape).astype(BF16)
    own_ref[...] = value.astype(BF16)


def weight_body(cols_ref, own_ref, other_ref, text_ref, out_ref):
    n_z, _, joint = out_ref.shape
    half = own_ref.shape[0]
    core = lax.axis_index("core")
    yh_id = lax.axis_index("yh")
    own_cols = cols_ref[pl.ds(pl.multiple_of(core * half, half), half), :]
    other_cols = cols_ref[pl.ds(pl.multiple_of((1 - core) * half, half), half), :]
    part = dot(own_cols, own_ref[...], ((0,), (0,))) + dot(other_cols, other_ref[...], ((0,), (0,)))
    n_text = text_ref.shape[0] // 2
    n_loc = n_text // n_z
    piece = part.shape[0] // n_z
    spare = out_ref.shape[1] - 2 * n_loc - piece
    here = text_ref[pl.ds(pl.multiple_of(yh_id * n_text, n_text), n_text), :].astype(F32)
    away = text_ref[pl.ds(pl.multiple_of((1 - yh_id) * n_text, n_text), n_text), :].astype(F32)
    for z in range(n_z):
        rows = jnp.concatenate(
            [
                here[z * n_loc : (z + 1) * n_loc],
                away[z * n_loc : (z + 1) * n_loc],
                part[z * piece : (z + 1) * piece],
                jnp.zeros((spare, joint), F32),
            ],
            axis=0,
        )
        out_ref[z] = rows.astype(BF16)


def z_sum_body(got_ref, here_ref, away_ref):
    total = jnp.sum(got_ref[...].astype(F32), axis=0)
    n_loc = here_ref.shape[0] // 2
    piece = total[2 * n_loc :]
    here_ref[...] = jnp.concatenate([total[:n_loc], piece], axis=0)
    away_ref[...] = jnp.concatenate([total[n_loc : 2 * n_loc], piece], axis=0).astype(BF16)


def yh_sum_body(here_ref, got_ref, text_ref, out_ref, d_texts_ref):
    total = here_ref[...] + got_ref[...].astype(F32)
    n_loc = text_ref.shape[0]
    unit, norm = unit_rows(text_ref[...].astype(F32))
    d_text = total[:n_loc]
    d_texts_ref[...] = (d_text - unit * jnp.sum(unit * d_text, axis=1, keepdims=True)) / norm
    out_ref[...] = jnp.broadcast_to(total[None, n_loc:], out_ref.shape)


def last_body(piece, got_ref, out_ref):
    rows = [got_ref[z, :piece, :] for z in range(got_ref.shape[0])]
    out_ref[...] = jnp.concatenate(rows, axis=0)[: out_ref.shape[0]]


def shards(clip_embed, clip_counts, pool_query, proj_weight, text_embed, pair_index, logit_scale):
    n_loc, n_clips, width = clip_embed.shape
    w_rows, joint = proj_weight.shape
    n_dp, n_yh, n_z = lax.axis_size(DP), lax.axis_size("yh"), lax.axis_size("z")
    n_yl, n_x, n_clip = lax.axis_size("yl"), lax.axis_size("x"), lax.axis_size(CLIP)
    n_plane = n_yl * n_x
    group_rows = n_loc * n_clip
    half = group_rows // 2
    n_lane = n_dp * n_loc
    core_id = lax.axis_index("core")
    plane_id = lax.axis_index(PLANE)
    lane_id = lax.axis_index(CLIP)
    group_id = lax.axis_index(DP)
    (text_send,) = local(text_body, [((n_dp, n_loc, joint), BF16)], 0, 1)(text_embed)
    text_own = exchange(text_send, DP).reshape(n_lane, joint)
    text_other = lax.ppermute(text_own, "core", SWAP)

    w_pad = -(-w_rows // 16) * 16
    query = pool_query.reshape(1, width)
    stage = [
        pltpu.SMEM((n_loc,), jnp.int32),
        pltpu.VMEM((n_loc, n_clips, width), BF16),
    ]
    (payload,) = local(
        pool_body,
        [((w_pad + 2 * n_loc, joint), BF16)],
        0,
        1,
        3,
        scratch=stage + [pltpu.VMEM((w_rows, joint), BF16), pltpu.SemaphoreType.DMA((3,))],
    )(query, clip_counts, clip_embed, proj_weight)

    near = [payload] + [
        lax.ppermute(payload, "yl", [(i, i ^ k) for i in range(n_yl)]) for k in range(1, n_yl)
    ]
    over_y = jnp.stack(near)
    over_y, text_own, text_other = lax.optimization_barrier((over_y, text_own, text_other))
    over_x = exchange(jnp.broadcast_to(over_y[None], (n_x, *over_y.shape)), "x")

    pairs = pair_index.reshape(n_dp, group_rows)
    over_x_other = lax.ppermute(over_x, "core", SWAP)

    full_weight, summaries, video_b, unit_own, norm_own, expo, row_send, col_send = local(
        functools.partial(logits_body, n_loc, w_rows),
        [
            ((width, joint), BF16),
            ((group_rows, width), BF16),
            ((group_rows, joint), BF16),
            ((n_loc, joint), F32),
            ((n_loc, 128), F32),
            ((group_rows, 2 * n_lane), F32),
            ((n_plane, 1, group_rows), F32),
            ((n_dp, 1, 2 * n_lane), F32),
        ],
        1,
        5,
        scratch=[
            pltpu.VMEM((width, joint), F32),
            pltpu.VMEM((group_rows, width), F32),
            pltpu.VMEM((group_rows, joint), F32),
            pltpu.VMEM((group_rows, 128), F32),
        ],
        flops=7e8,
        moved=8e6,
        mib=20,
    )(logit_scale, over_x, over_x_other, text_own, text_other, pairs)
    rows = exchange(row_send, PLANE)
    cols = exchange(col_send, DP)

    video_part, text_part = local(
        functools.partial(grad_body, n_loc, n_clip),
        [((half, joint), BF16), ((n_lane, joint), BF16)],
        1,
        7,
        scratch=[pltpu.VMEM((group_rows, 2 * n_lane), BF16)],
        flops=2e8,
    )(logit_scale, expo, rows, cols, pairs, text_own, text_other, video_b)

    got_video = exchange(video_part.reshape(n_plane, n_loc, joint), PLANE)
    d_send, d_own = local(
        projected_body, [((n_plane, n_loc, joint), BF16), ((n_loc, joint), BF16)], 0, 3
    )(got_video, unit_own, norm_own)
    d_half, d_own = lax.optimization_barrier((exchange(d_send, PLANE).reshape(half, joint), d_own))
    d_half_other = lax.ppermute(d_half, "core", SWAP)

    summary_cols = lax.dynamic_slice(summaries, (0, lane_id * w_rows), (group_rows, w_rows))
    summary_cols = jnp.pad(summary_cols, ((0, 0), (0, w_pad - w_rows)))
    d_half, summary_cols = lax.optimization_barrier((d_half, summary_cols))
    piece = w_pad // n_z
    spare = -(-piece // 8) * 8
    (parts,) = local(weight_body, [((n_z, 2 * n_loc + spare, joint), BF16)], 0, 4, flops=3e7)(
        summary_cols, d_half, d_half_other, text_part
    )
    got_z, d_own = lax.optimization_barrier((exchange(parts, "z"), d_own))
    here, away = local(
        z_sum_body, [((n_loc + spare, joint), F32), ((n_loc + spare, joint), BF16)], 0, 1
    )(got_z)
    got_yh = lax.ppermute(away, "yh", SWAP)

    (d_clips,) = local(
        clips_body,
        [((n_loc, n_clips, width), BF16)],
        0,
        2,
        3,
        scratch=stage + [pltpu.VMEM((width, joint), BF16), pltpu.SemaphoreType.DMA((3,))],
        flops=2e7,
        moved=3e6,
    )(d_own, query, clip_counts, clip_embed, full_weight)
    piece_send, d_texts = local(
        yh_sum_body, [((n_z, spare, joint), F32), ((n_loc, joint), F32)], 0, 3
    )(here, got_yh, text_embed)
    piece_send, d_clips = lax.optimization_barrier((piece_send, d_clips))
    (d_weight,) = local(functools.partial(last_body, piece), [((w_rows, joint), F32)], 0, 1)(
        exchange(piece_send, "z")
    )
    return (d_clips, d_weight, d_texts)


def solution(mesh):
    fine = Mesh(mesh.devices.reshape(2, 8, 4, 4, 2), DP + CLIP)
    everywhere = DP + CLIP
    return jax.shard_map(
        shards,
        mesh=fine,
        in_specs=(
            P(everywhere, None, None),
            P(everywhere),
            P(),
            P(CLIP, None),
            P(everywhere, None),
            P(),
            P(),
        ),
        out_specs=(P(everywhere, None, None), P(CLIP, None), P(everywhere, None)),
        check_vma=False,
    )
```

```python
import functools

import jax
import jax.numpy as jnp
from jax import lax
from jax.experimental import pallas as pl
from jax.experimental.pallas import tpu as pltpu
from jax.sharding import Mesh, PartitionSpec as P

EPS = 1e-06
F32 = jnp.float32
BF16 = jnp.bfloat16
DP = ("yh", "z")
CLIP = ("yl", "x", "core")
PLANE = ("yl", "x")
SWAP = [(0, 1), (1, 0)]


def unit_rows(values):
    norm_value = jnp.sqrt(jnp.sum(values * values, axis=1, keepdims=True) + EPS)
    return (values / norm_value, norm_value)


def exchange(blocks, axes):
    return lax.all_to_all(blocks, axes, split_axis=0, concat_axis=0, tiled=True)


def dot(a, b, contract):
    return lax.dot_general(a, b, (contract, ((), ())), preferred_element_type=F32)


def local(body, outs, n_scalars, n_args, n_far=0, scratch=(), flops=1e6, moved=1e6, mib=8):
    vmem = pl.BlockSpec(memory_space=pltpu.VMEM)
    smem = pl.BlockSpec(memory_space=pltpu.SMEM)
    far = pl.BlockSpec(memory_space=pltpu.HBM)
    return pl.pallas_call(
        body,
        out_shape=tuple(jax.ShapeDtypeStruct(shape, dtype) for shape, dtype in outs),
        in_specs=[smem] * n_scalars + [vmem] * n_args + [far] * n_far,
        out_specs=tuple(vmem for _ in outs),
        scratch_shapes=list(scratch),
        compiler_params=pltpu.CompilerParams(vmem_limit_bytes=mib * 1024 * 1024),
        cost_estimate=pl.CostEstimate(flops=int(flops), bytes_accessed=int(moved), transcendentals=0),
    )


def pool(counts_ref, embed, query):
    n_loc, n_clips, _ = embed.shape
    scores = jnp.sum(embed * query[None], axis=2, keepdims=True)
    video = lax.broadcasted_iota(jnp.int32, (n_loc, n_clips, 1), 0)
    clip = lax.broadcasted_iota(jnp.int32, (n_loc, n_clips, 1), 1)
    count = jnp.zeros((n_loc, n_clips, 1), jnp.int32)
    for v in range(n_loc):
        count = jnp.where(video == v, counts_ref[v], count)
    usable = clip < count
    masked = jnp.where(usable, scores, -1e30)
    raised = jnp.where(usable, jnp.exp(masked - jnp.max(masked, axis=1, keepdims=True)), 0.0)
    weights = raised / jnp.sum(raised, axis=1, keepdims=True)
    return weights, jnp.sum(weights * embed, axis=1)


def fetch(sources, targets, sems):
    copies = [
        pltpu.make_async_copy(source, target, sems.at[i])
        for i, (source, target) in enumerate(zip(sources, targets))
    ]
    for copy in copies:
        copy.start()
    for copy in copies:
        copy.wait()


def pool_body(
    query_hbm, counts_hbm, clips_hbm, rows_hbm, text_hbm, payload_ref, send_ref,
    query_ref, counts_ref, clips_ref, rows_ref, text_ref, sems,
):
    fetch(
        (query_hbm, counts_hbm, clips_hbm, rows_hbm, text_hbm),
        (query_ref, counts_ref, clips_ref, rows_ref, text_ref),
        sems,
    )
    unit, _ = unit_rows(text_ref[...].astype(F32))
    send_ref[...] = jnp.broadcast_to(unit[None], send_ref.shape).astype(BF16)
    n_loc, _, width = clips_ref.shape
    w_rows, joint = rows_ref.shape
    w_pad = payload_ref.shape[0] - 2 * n_loc
    _, summary = pool(counts_ref, clips_ref[...].astype(F32), query_ref[...].astype(F32).reshape(1, width))
    high = jnp.concatenate(
        [summary[:, joint:], jnp.zeros((n_loc, 2 * joint - width), F32)], axis=1
    )
    tail = jnp.zeros((w_pad - w_rows, joint), F32)
    payload_ref[...] = jnp.concatenate(
        [rows_ref[...].astype(F32), tail, summary[:, :joint], high], axis=0
    ).astype(BF16)


def clips_body(
    d_own_ref, query_hbm, counts_hbm, clips_hbm, weight_hbm, out_ref,
    query_ref, counts_ref, clips_ref, weight_ref, sems,
):
    fetch(
        (query_hbm, counts_hbm, clips_hbm, weight_hbm),
        (query_ref, counts_ref, clips_ref, weight_ref),
        sems,
    )
    embed = clips_ref[...].astype(F32)
    query = query_ref[...].astype(F32).reshape(1, embed.shape[2])
    weights, summary = pool(counts_ref, embed, query)
    d_summary = dot(d_own_ref[...], weight_ref[...], ((1,), (1,)))
    aligned = jnp.sum(embed * d_summary[:, None, :], axis=2, keepdims=True)
    baseline = jnp.sum(d_summary * summary, axis=1, keepdims=True)
    d_scores = weights * (aligned - baseline[:, None, :])
    out_ref[...] = (weights * d_summary[:, None, :] + d_scores * query[None]).astype(BF16)


def column(row):
    return jnp.broadcast_to(row, (128, row.shape[1])).T[:, :1]


def logits_body(
    n_loc, w_rows, scale_ref, own_ref, other_ref, text_own_ref, text_other_ref,
    _, weight_ref, summary_ref, video_ref, unit_ref, norm_ref, expo_ref, rows_ref, cols_ref,
    weight_f, summary_f, unit_f, norm_f,
):
    n_x, n_yl, _, joint = own_ref.shape
    width = weight_ref.shape[0]
    half = n_x * n_yl * n_loc
    w_pad = -(-w_rows // 16) * 16
    first = lax.axis_index("core") == 0
    yl_id = lax.axis_index("yl")
    for x in range(n_x):
        for yl in range(n_yl):
            slot = jnp.bitwise_xor(yl_id, yl)
            own = own_ref[x, slot].astype(F32)
            other = other_ref[x, slot].astype(F32)
            pair = (jnp.where(first, own, other), jnp.where(first, other, own))
            for core in range(2):
                at = ((yl * n_x + x) * 2 + core) * w_rows
                weight_f[at : at + w_rows, :] = pair[core][:w_rows]
                row = core * half + (yl * n_x + x) * n_loc
                summary_f[row : row + n_loc, :joint] = pair[core][w_pad : w_pad + n_loc]
                summary_f[row : row + n_loc, joint:] = pair[core][w_pad + n_loc :, : width - joint]
    weight_b = weight_f[...].astype(BF16)
    summary_b = summary_f[...].astype(BF16)
    weight_ref[...] = weight_b
    summary_ref[...] = summary_b
    unit, norm = unit_rows(dot(summary_b, weight_b, ((1,), (0,))))
    video_b = unit.astype(BF16)
    video_ref[...] = video_b
    unit_f[...] = unit
    norm_f[...] = jnp.broadcast_to(norm, norm_f.shape)
    place = (lax.axis_index("core") * n_yl + yl_id) * n_x + lax.axis_index("x")
    mine = pl.ds(pl.multiple_of(place * n_loc, n_loc), n_loc)
    unit_ref[...] = unit_f[mine, :]
    norm_ref[...] = norm_f[mine, :]
    n_lane = text_own_ref.shape[0]
    scale = scale_ref[0]
    expo_ref[:, :n_lane] = jnp.exp(scale * dot(video_b, text_own_ref[...], ((1,), (1,))))
    expo_ref[:, n_lane:] = jnp.exp(scale * dot(video_b, text_other_ref[...], ((1,), (1,))))
    expo = expo_ref[...]
    row_part = jnp.broadcast_to(jnp.sum(expo, axis=1, keepdims=True), (2 * half, 128)).T[:1]
    col_part = jnp.sum(expo, axis=0, keepdims=True)
    rows_ref[...] = jnp.broadcast_to(row_part[None], rows_ref.shape)
    cols_ref[...] = jnp.broadcast_to(col_part[None], cols_ref.shape)


def grad_body(
    n_loc, n_clip, scale_ref, expo_ref, rows_ref, cols_ref, pairs_ref, text_own_ref,
    text_other_ref, video_ref, part_ref, text_part_ref, grad_ref,
):
    n_lane = text_own_ref.shape[0]
    rows = jnp.sum(rows_ref[...], axis=0)
    cols = jnp.sum(cols_ref[...], axis=0)
    core = lax.axis_index("core")
    plane = lax.axis_index("yl") * lax.axis_size("x") + lax.axis_index("x")
    at = lax.broadcasted_iota(jnp.int32, (1, 2 * n_lane), 1)
    lane = jnp.where(at < n_lane, plane * 2 + core, plane * 2 + (1 - core))
    slot = jnp.where(at < n_lane, at, at - n_lane)
    col_id = ((slot // n_loc) * n_clip + lane) * n_loc + slot % n_loc
    group = lax.axis_index("yh") * lax.axis_size("z") + lax.axis_index("z")
    pairs = column(pairs_ref[pl.ds(group, 1), :].astype(F32)).astype(jnp.int32)
    pairs = pairs.reshape(-1, 2, n_loc, 1)
    pairs = jnp.concatenate([pairs[:, 0], pairs[:, 1]], axis=0).reshape(-1, 1)
    positive = jnp.where(pairs == col_id, 1.0, 0.0)
    expo = expo_ref[...]
    grad = (expo / column(rows) + expo / cols) * 0.5 - positive
    grad_ref[...] = grad.astype(BF16)
    half = expo.shape[0] // 2
    mine = grad_ref[pl.ds(pl.multiple_of(core * half, half), half), :]
    part = dot(mine[:, :n_lane], text_own_ref[...], ((1,), (0,)))
    part = part + dot(mine[:, n_lane:], text_other_ref[...], ((1,), (0,)))
    part_ref[...] = (scale_ref[0] * part).astype(BF16)
    text_part = dot(grad_ref[:, :n_lane], video_ref[...], ((0,), (0,)))
    text_part_ref[...] = (scale_ref[0] * text_part).astype(BF16)


def projected_body(part_ref, unit_ref, norm_ref, out_ref, own_ref):
    d_video = jnp.sum(part_ref[...].astype(F32), axis=0)
    unit = unit_ref[...]
    norm = norm_ref[:, :1]
    value = (d_video - unit * jnp.sum(unit * d_video, axis=1, keepdims=True)) / norm
    out_ref[...] = jnp.broadcast_to(value[None], out_ref.shape).astype(BF16)
    own_ref[...] = value.astype(BF16)


def weight_body(cols_ref, own_ref, other_ref, text_ref, out_ref):
    n_z, _, joint = out_ref.shape
    half = own_ref.shape[0]
    core = lax.axis_index("core")
    yh_id = lax.axis_index("yh")
    own_cols = cols_ref[pl.ds(pl.multiple_of(core * half, half), half), :]
    other_cols = cols_ref[pl.ds(pl.multiple_of((1 - core) * half, half), half), :]
    part = dot(own_cols, own_ref[...], ((0,), (0,))) + dot(other_cols, other_ref[...], ((0,), (0,)))
    n_text = text_ref.shape[0] // 2
    n_loc = n_text // n_z
    piece = part.shape[0] // n_z
    spare = out_ref.shape[1] - 2 * n_loc - piece
    here = text_ref[pl.ds(pl.multiple_of(yh_id * n_text, n_text), n_text), :].astype(F32)
    away = text_ref[pl.ds(pl.multiple_of((1 - yh_id) * n_text, n_text), n_text), :].astype(F32)
    for z in range(n_z):
        rows = jnp.concatenate(
            [
                here[z * n_loc : (z + 1) * n_loc],
                away[z * n_loc : (z + 1) * n_loc],
                part[z * piece : (z + 1) * piece],
                jnp.zeros((spare, joint), F32),
            ],
            axis=0,
        )
        out_ref[z] = rows.astype(BF16)


def z_sum_body(got_ref, here_ref, away_ref):
    total = jnp.sum(got_ref[...].astype(F32), axis=0)
    n_loc = here_ref.shape[0] // 2
    piece = total[2 * n_loc :]
    here_ref[...] = jnp.concatenate([total[:n_loc], piece], axis=0)
    away_ref[...] = jnp.concatenate([total[n_loc : 2 * n_loc], piece], axis=0).astype(BF16)


def yh_sum_body(here_ref, got_ref, text_ref, out_ref, d_texts_ref):
    total = here_ref[...] + got_ref[...].astype(F32)
    n_loc = text_ref.shape[0]
    unit, norm = unit_rows(text_ref[...].astype(F32))
    d_text = total[:n_loc]
    d_texts_ref[...] = (d_text - unit * jnp.sum(unit * d_text, axis=1, keepdims=True)) / norm
    out_ref[...] = jnp.broadcast_to(total[None, n_loc:], out_ref.shape)


def last_body(piece, got_ref, out_ref):
    rows = [got_ref[z, :piece, :] for z in range(got_ref.shape[0])]
    out_ref[...] = jnp.concatenate(rows, axis=0)[: out_ref.shape[0]]


def shards(clip_embed, clip_counts, pool_query, proj_weight, text_embed, pair_index, logit_scale):
    n_loc, n_clips, width = clip_embed.shape
    w_rows, joint = proj_weight.shape
    n_dp, n_yh, n_z = lax.axis_size(DP), lax.axis_size("yh"), lax.axis_size("z")
    n_yl, n_x, n_clip = lax.axis_size("yl"), lax.axis_size("x"), lax.axis_size(CLIP)
    n_plane = n_yl * n_x
    group_rows = n_loc * n_clip
    half = group_rows // 2
    n_lane = n_dp * n_loc
    core_id = lax.axis_index("core")
    plane_id = lax.axis_index(PLANE)
    lane_id = lax.axis_index(CLIP)
    group_id = lax.axis_index(DP)
    w_pad = -(-w_rows // 16) * 16
    stage = [
        pltpu.VMEM((width,), BF16),
        pltpu.SMEM((n_loc,), jnp.int32),
        pltpu.VMEM((n_loc, n_clips, width), BF16),
    ]
    payload, text_send = local(
        pool_body,
        [((w_pad + 2 * n_loc, joint), BF16), ((n_dp, n_loc, joint), BF16)],
        0,
        0,
        5,
        scratch=stage
        + [
            pltpu.VMEM((w_rows, joint), BF16),
            pltpu.VMEM((n_loc, joint), BF16),
            pltpu.SemaphoreType.DMA((5,)),
        ],
        mib=56,
    )(pool_query, clip_counts, clip_embed, proj_weight, text_embed)
    text_own = exchange(text_send, DP).reshape(n_lane, joint)
    text_other = lax.ppermute(text_own, "core", SWAP)

    near = [payload] + [
        lax.ppermute(payload, "yl", [(i, i ^ k) for i in range(n_yl)]) for k in range(1, n_yl)
    ]
    over_y = jnp.stack(near)
    over_y, text_own, text_other = lax.optimization_barrier((over_y, text_own, text_other))
    over_x = exchange(jnp.broadcast_to(over_y[None], (n_x, *over_y.shape)), "x")

    pairs = pair_index.reshape(n_dp, group_rows)
    over_x_other = lax.ppermute(over_x, "core", SWAP)

    full_weight, summaries, video_b, unit_own, norm_own, expo, row_send, col_send = local(
        functools.partial(logits_body, n_loc, w_rows),
        [
            ((width, joint), BF16),
            ((group_rows, width), BF16),
            ((group_rows, joint), BF16),
            ((n_loc, joint), F32),
            ((n_loc, 128), F32),
            ((group_rows, 2 * n_lane), F32),
            ((n_plane, 1, group_rows), F32),
            ((n_dp, 1, 2 * n_lane), F32),
        ],
        1,
        5,
        scratch=[
            pltpu.VMEM((width, joint), F32),
            pltpu.VMEM((group_rows, width), F32),
            pltpu.VMEM((group_rows, joint), F32),
            pltpu.VMEM((group_rows, 128), F32),
        ],
        flops=7e8,
        moved=8e6,
        mib=20,
    )(logit_scale, over_x, over_x_other, text_own, text_other, pairs)
    rows = exchange(row_send, PLANE)
    cols = exchange(col_send, DP)

    video_part, text_part = local(
        functools.partial(grad_body, n_loc, n_clip),
        [((half, joint), BF16), ((n_lane, joint), BF16)],
        1,
        7,
        scratch=[pltpu.VMEM((group_rows, 2 * n_lane), BF16)],
        flops=2e8,
    )(logit_scale, expo, rows, cols, pairs, text_own, text_other, video_b)

    got_video = exchange(video_part.reshape(n_plane, n_loc, joint), PLANE)
    d_send, d_own = local(
        projected_body, [((n_plane, n_loc, joint), BF16), ((n_loc, joint), BF16)], 0, 3
    )(got_video, unit_own, norm_own)
    d_half, d_own = lax.optimization_barrier((exchange(d_send, PLANE).reshape(half, joint), d_own))
    d_half_other = lax.ppermute(d_half, "core", SWAP)

    summary_cols = lax.dynamic_slice(summaries, (0, lane_id * w_rows), (group_rows, w_rows))
    summary_cols = jnp.pad(summary_cols, ((0, 0), (0, w_pad - w_rows)))
    d_half, summary_cols = lax.optimization_barrier((d_half, summary_cols))
    piece = w_pad // n_z
    spare = -(-piece // 8) * 8
    (parts,) = local(weight_body, [((n_z, 2 * n_loc + spare, joint), BF16)], 0, 4, flops=3e7)(
        summary_cols, d_half, d_half_other, text_part
    )
    got_z, d_own = lax.optimization_barrier((exchange(parts, "z"), d_own))
    here, away = local(
        z_sum_body, [((n_loc + spare, joint), F32), ((n_loc + spare, joint), BF16)], 0, 1
    )(got_z)
    got_yh = lax.ppermute(away, "yh", SWAP)

    (d_clips,) = local(
        clips_body,
        [((n_loc, n_clips, width), BF16)],
        0,
        1,
        4,
        scratch=stage + [pltpu.VMEM((width, joint), BF16), pltpu.SemaphoreType.DMA((4,))],
        flops=2e7,
        moved=3e6,
    )(d_own, pool_query, clip_counts, clip_embed, full_weight)
    piece_send, d_texts = local(
        yh_sum_body, [((n_z, spare, joint), F32), ((n_loc, joint), F32)], 0, 3
    )(here, got_yh, text_embed)
    piece_send, d_clips = lax.optimization_barrier((piece_send, d_clips))
    (d_weight,) = local(functools.partial(last_body, piece), [((w_rows, joint), F32)], 0, 1)(
        exchange(piece_send, "z")
    )
    return (d_clips, d_weight, d_texts)


def solution(mesh):
    fine = Mesh(mesh.devices.reshape(2, 8, 4, 4, 2), DP + CLIP)
    everywhere = DP + CLIP
    return jax.shard_map(
        shards,
        mesh=fine,
        in_specs=(
            P(everywhere, None, None),
            P(everywhere),
            P(),
            P(CLIP, None),
            P(everywhere, None),
            P(),
            P(),
        ),
        out_specs=(P(everywhere, None, None), P(CLIP, None), P(everywhere, None)),
        check_vma=False,
    )
```

```python
import functools

import jax
import jax.numpy as jnp
from jax import lax
from jax.experimental import pallas as pl
from jax.experimental.pallas import tpu as pltpu
from jax.sharding import Mesh, PartitionSpec as P

EPS = 1e-06
F32 = jnp.float32
BF16 = jnp.bfloat16
DP = ("yh", "z")
CLIP = ("yl", "x", "core")
PLANE = ("yl", "x")
SWAP = [(0, 1), (1, 0)]


def unit_rows(values):
    norm_value = jnp.sqrt(jnp.sum(values * values, axis=1, keepdims=True) + EPS)
    return (values / norm_value, norm_value)


def exchange(blocks, axes):
    return lax.all_to_all(blocks, axes, split_axis=0, concat_axis=0, tiled=True)


def dot(a, b, contract):
    return lax.dot_general(a, b, (contract, ((), ())), preferred_element_type=F32)


def local(body, outs, n_scalars, n_args, n_far=0, scratch=(), flops=1e6, moved=1e6, mib=8):
    vmem = pl.BlockSpec(memory_space=pltpu.VMEM)
    smem = pl.BlockSpec(memory_space=pltpu.SMEM)
    far = pl.BlockSpec(memory_space=pltpu.HBM)
    return pl.pallas_call(
        body,
        out_shape=tuple(jax.ShapeDtypeStruct(shape, dtype) for shape, dtype in outs),
        in_specs=[smem] * n_scalars + [vmem] * n_args + [far] * n_far,
        out_specs=tuple(vmem for _ in outs),
        scratch_shapes=list(scratch),
        compiler_params=pltpu.CompilerParams(vmem_limit_bytes=mib * 1024 * 1024),
        cost_estimate=pl.CostEstimate(flops=int(flops), bytes_accessed=int(moved), transcendentals=0),
    )


def pool(counts_ref, embed, query):
    n_loc, n_clips, _ = embed.shape
    scores = jnp.sum(embed * query[None], axis=2, keepdims=True)
    video = lax.broadcasted_iota(jnp.int32, (n_loc, n_clips, 1), 0)
    clip = lax.broadcasted_iota(jnp.int32, (n_loc, n_clips, 1), 1)
    count = jnp.zeros((n_loc, n_clips, 1), jnp.int32)
    for v in range(n_loc):
        count = jnp.where(video == v, counts_ref[v], count)
    usable = clip < count
    masked = jnp.where(usable, scores, -1e30)
    raised = jnp.where(usable, jnp.exp(masked - jnp.max(masked, axis=1, keepdims=True)), 0.0)
    weights = raised / jnp.sum(raised, axis=1, keepdims=True)
    return weights, jnp.sum(weights * embed, axis=1)


def fetch(sources, targets, sems):
    copies = [
        pltpu.make_async_copy(source, target, sems.at[i])
        for i, (source, target) in enumerate(zip(sources, targets))
    ]
    for copy in copies:
        copy.start()
    for copy in copies:
        copy.wait()


def pool_body(
    query_hbm, counts_hbm, clips_hbm, rows_hbm, text_hbm, payload_ref, send_ref,
    query_ref, counts_ref, clips_ref, rows_ref, text_ref, sems,
):
    fetch(
        (query_hbm, counts_hbm, clips_hbm, rows_hbm, text_hbm),
        (query_ref, counts_ref, clips_ref, rows_ref, text_ref),
        sems,
    )
    unit, _ = unit_rows(text_ref[...].astype(F32))
    send_ref[...] = jnp.broadcast_to(unit[None], send_ref.shape).astype(BF16)
    n_loc, _, width = clips_ref.shape
    w_rows, joint = rows_ref.shape
    w_pad = payload_ref.shape[0] - 2 * n_loc
    _, summary = pool(counts_ref, clips_ref[...].astype(F32), query_ref[...].astype(F32).reshape(1, width))
    high = jnp.concatenate(
        [summary[:, joint:], jnp.zeros((n_loc, 2 * joint - width), F32)], axis=1
    )
    tail = jnp.zeros((w_pad - w_rows, joint), F32)
    payload_ref[...] = jnp.concatenate(
        [rows_ref[...].astype(F32), tail, summary[:, :joint], high], axis=0
    ).astype(BF16)


def clips_body(
    d_own_ref, query_hbm, counts_hbm, clips_hbm, weight_hbm, out_ref,
    query_ref, counts_ref, clips_ref, weight_ref, sems,
):
    fetch(
        (query_hbm, counts_hbm, clips_hbm, weight_hbm),
        (query_ref, counts_ref, clips_ref, weight_ref),
        sems,
    )
    embed = clips_ref[...].astype(F32)
    query = query_ref[...].astype(F32).reshape(1, embed.shape[2])
    weights, summary = pool(counts_ref, embed, query)
    d_summary = dot(d_own_ref[...], weight_ref[...], ((1,), (1,)))
    aligned = jnp.sum(embed * d_summary[:, None, :], axis=2, keepdims=True)
    baseline = jnp.sum(d_summary * summary, axis=1, keepdims=True)
    d_scores = weights * (aligned - baseline[:, None, :])
    out_ref[...] = (weights * d_summary[:, None, :] + d_scores * query[None]).astype(BF16)


def column(row):
    return jnp.broadcast_to(row, (128, row.shape[1])).T[:, :1]


def logits_body(
    n_loc, w_rows, scale_ref, own_ref, other_ref, text_own_ref, text_other_ref,
    _, weight_ref, summary_ref, video_ref, unit_ref, norm_ref, expo_ref, send_ref,
    weight_f, summary_f, unit_f, norm_f,
):
    n_x, n_yl, _, joint = own_ref.shape
    width = weight_ref.shape[0]
    half = n_x * n_yl * n_loc
    w_pad = -(-w_rows // 16) * 16
    first = lax.axis_index("core") == 0
    yl_id = lax.axis_index("yl")
    for x in range(n_x):
        for yl in range(n_yl):
            slot = jnp.bitwise_xor(yl_id, yl)
            own = own_ref[x, slot].astype(F32)
            other = other_ref[x, slot].astype(F32)
            pair = (jnp.where(first, own, other), jnp.where(first, other, own))
            for core in range(2):
                at = ((yl * n_x + x) * 2 + core) * w_rows
                weight_f[at : at + w_rows, :] = pair[core][:w_rows]
                row = core * half + (yl * n_x + x) * n_loc
                summary_f[row : row + n_loc, :joint] = pair[core][w_pad : w_pad + n_loc]
                summary_f[row : row + n_loc, joint:] = pair[core][w_pad + n_loc :, : width - joint]
    weight_b = weight_f[...].astype(BF16)
    summary_b = summary_f[...].astype(BF16)
    weight_ref[...] = weight_b
    summary_ref[...] = summary_b
    unit, norm = unit_rows(dot(summary_b, weight_b, ((1,), (0,))))
    video_b = unit.astype(BF16)
    video_ref[...] = video_b
    unit_f[...] = unit
    norm_f[...] = jnp.broadcast_to(norm, norm_f.shape)
    place = (lax.axis_index("core") * n_yl + yl_id) * n_x + lax.axis_index("x")
    mine = pl.ds(pl.multiple_of(place * n_loc, n_loc), n_loc)
    unit_ref[...] = unit_f[mine, :]
    norm_ref[...] = norm_f[mine, :]
    n_lane = text_own_ref.shape[0]
    scale = scale_ref[0]
    expo_ref[:, :n_lane] = jnp.exp(scale * dot(video_b, text_own_ref[...], ((1,), (1,))))
    expo_ref[:, n_lane:] = jnp.exp(scale * dot(video_b, text_other_ref[...], ((1,), (1,))))
    expo = expo_ref[...]
    row_part = jnp.broadcast_to(jnp.sum(expo, axis=1, keepdims=True), (2 * half, 128)).T[:1]
    col_part = jnp.sum(expo, axis=0, keepdims=True)
    send_ref[...] = jnp.broadcast_to(jnp.where(first, row_part, col_part)[None], send_ref.shape)


def totals_body(got_ref, out_ref):
    out_ref[...] = jnp.broadcast_to(jnp.sum(got_ref[...], axis=0), out_ref.shape)


def grad_body(
    n_loc, n_clip, scale_ref, expo_ref, totals_ref, totals_other_ref, pairs_ref, text_own_ref,
    text_other_ref, video_ref, part_ref, text_part_ref, grad_ref,
):
    n_lane = text_own_ref.shape[0]
    own = totals_ref[:1]
    other = totals_other_ref[:1]
    first = lax.axis_index("core") == 0
    swapped = jnp.concatenate([other[:, n_lane:], other[:, :n_lane]], axis=1)
    rows = jnp.where(first, own, other)
    cols = jnp.where(first, swapped, own)
    core = lax.axis_index("core")
    plane = lax.axis_index("yl") * lax.axis_size("x") + lax.axis_index("x")
    at = lax.broadcasted_iota(jnp.int32, (1, 2 * n_lane), 1)
    lane = jnp.where(at < n_lane, plane * 2 + core, plane * 2 + (1 - core))
    slot = jnp.where(at < n_lane, at, at - n_lane)
    col_id = ((slot // n_loc) * n_clip + lane) * n_loc + slot % n_loc
    group = lax.axis_index("yh") * lax.axis_size("z") + lax.axis_index("z")
    pairs = column(pairs_ref[pl.ds(group, 1), :].astype(F32)).astype(jnp.int32)
    pairs = pairs.reshape(-1, 2, n_loc, 1)
    pairs = jnp.concatenate([pairs[:, 0], pairs[:, 1]], axis=0).reshape(-1, 1)
    positive = jnp.where(pairs == col_id, 1.0, 0.0)
    expo = expo_ref[...]
    grad = (expo / column(rows) + expo / cols) * 0.5 - positive
    grad_ref[...] = grad.astype(BF16)
    half = expo.shape[0] // 2
    mine = grad_ref[pl.ds(pl.multiple_of(core * half, half), half), :]
    part = dot(mine[:, :n_lane], text_own_ref[...], ((1,), (0,)))
    part = part + dot(mine[:, n_lane:], text_other_ref[...], ((1,), (0,)))
    part_ref[...] = (scale_ref[0] * part).astype(BF16)
    text_part = dot(grad_ref[:, :n_lane], video_ref[...], ((0,), (0,)))
    text_part_ref[...] = (scale_ref[0] * text_part).astype(BF16)


def projected_body(part_ref, unit_ref, norm_ref, out_ref, own_ref):
    d_video = jnp.sum(part_ref[...].astype(F32), axis=0)
    unit = unit_ref[...]
    norm = norm_ref[:, :1]
    value = (d_video - unit * jnp.sum(unit * d_video, axis=1, keepdims=True)) / norm
    out_ref[...] = jnp.broadcast_to(value[None], out_ref.shape).astype(BF16)
    own_ref[...] = value.astype(BF16)


def weight_body(cols_ref, own_ref, other_ref, text_ref, out_ref):
    n_z, _, joint = out_ref.shape
    half = own_ref.shape[0]
    core = lax.axis_index("core")
    yh_id = lax.axis_index("yh")
    own_cols = cols_ref[pl.ds(pl.multiple_of(core * half, half), half), :]
    other_cols = cols_ref[pl.ds(pl.multiple_of((1 - core) * half, half), half), :]
    part = dot(own_cols, own_ref[...], ((0,), (0,))) + dot(other_cols, other_ref[...], ((0,), (0,)))
    n_text = text_ref.shape[0] // 2
    n_loc = n_text // n_z
    piece = part.shape[0] // n_z
    spare = out_ref.shape[1] - 2 * n_loc - piece
    here = text_ref[pl.ds(pl.multiple_of(yh_id * n_text, n_text), n_text), :].astype(F32)
    away = text_ref[pl.ds(pl.multiple_of((1 - yh_id) * n_text, n_text), n_text), :].astype(F32)
    for z in range(n_z):
        rows = jnp.concatenate(
            [
                here[z * n_loc : (z + 1) * n_loc],
                away[z * n_loc : (z + 1) * n_loc],
                part[z * piece : (z + 1) * piece],
                jnp.zeros((spare, joint), F32),
            ],
            axis=0,
        )
        out_ref[z] = rows.astype(BF16)


def z_sum_body(got_ref, here_ref, away_ref):
    total = jnp.sum(got_ref[...].astype(F32), axis=0)
    n_loc = here_ref.shape[0] // 2
    piece = total[2 * n_loc :]
    here_ref[...] = jnp.concatenate([total[:n_loc], piece], axis=0)
    away_ref[...] = jnp.concatenate([total[n_loc : 2 * n_loc], piece], axis=0).astype(BF16)


def yh_sum_body(n_loc, here_ref, got_ref, out_ref, text_ref):
    total = here_ref[...] + got_ref[...].astype(F32)
    text_ref[...] = total[:n_loc]
    out_ref[...] = jnp.broadcast_to(total[None, n_loc:], out_ref.shape)


def last_body(piece, got_ref, d_text_ref, text_ref, out_ref, d_texts_ref):
    rows = [got_ref[z, :piece, :] for z in range(got_ref.shape[0])]
    out_ref[...] = jnp.concatenate(rows, axis=0)[: out_ref.shape[0]]
    unit, norm = unit_rows(text_ref[...].astype(F32))
    d_text = d_text_ref[...]
    d_texts_ref[...] = (d_text - unit * jnp.sum(unit * d_text, axis=1, keepdims=True)) / norm


def shards(clip_embed, clip_counts, pool_query, proj_weight, text_embed, pair_index, logit_scale):
    n_loc, n_clips, width = clip_embed.shape
    w_rows, joint = proj_weight.shape
    n_dp, n_yh, n_z = lax.axis_size(DP), lax.axis_size("yh"), lax.axis_size("z")
    n_yl, n_x, n_clip = lax.axis_size("yl"), lax.axis_size("x"), lax.axis_size(CLIP)
    n_plane = n_yl * n_x
    group_rows = n_loc * n_clip
    half = group_rows // 2
    n_lane = n_dp * n_loc
    core_id = lax.axis_index("core")
    plane_id = lax.axis_index(PLANE)
    lane_id = lax.axis_index(CLIP)
    group_id = lax.axis_index(DP)
    w_pad = -(-w_rows // 16) * 16
    stage = [
        pltpu.VMEM((width,), BF16),
        pltpu.SMEM((n_loc,), jnp.int32),
        pltpu.VMEM((n_loc, n_clips, width), BF16),
    ]
    payload, text_send = local(
        pool_body,
        [((w_pad + 2 * n_loc, joint), BF16), ((n_dp, n_loc, joint), BF16)],
        0,
        0,
        5,
        scratch=stage
        + [
            pltpu.VMEM((w_rows, joint), BF16),
            pltpu.VMEM((n_loc, joint), BF16),
            pltpu.SemaphoreType.DMA((5,)),
        ],
        mib=56,
    )(pool_query, clip_counts, clip_embed, proj_weight, text_embed)
    text_own = exchange(text_send, DP).reshape(n_lane, joint)
    text_other = lax.ppermute(text_own, "core", SWAP)

    near = [payload] + [
        lax.ppermute(payload, "yl", [(i, i ^ k) for i in range(n_yl)]) for k in range(1, n_yl)
    ]
    over_y = jnp.stack(near)
    over_y, text_own, text_other = lax.optimization_barrier((over_y, text_own, text_other))
    over_x = exchange(jnp.broadcast_to(over_y[None], (n_x, *over_y.shape)), "x")

    pairs = pair_index.reshape(n_dp, group_rows)
    over_x_other = lax.ppermute(over_x, "core", SWAP)

    full_weight, summaries, video_b, unit_own, norm_own, expo, totals_send = local(
        functools.partial(logits_body, n_loc, w_rows),
        [
            ((width, joint), BF16),
            ((group_rows, width), BF16),
            ((group_rows, joint), BF16),
            ((n_loc, joint), F32),
            ((n_loc, 128), F32),
            ((group_rows, 2 * n_lane), F32),
            ((n_plane, 1, group_rows), F32),
        ],
        1,
        5,
        scratch=[
            pltpu.VMEM((width, joint), F32),
            pltpu.VMEM((group_rows, width), F32),
            pltpu.VMEM((group_rows, joint), F32),
            pltpu.VMEM((group_rows, 128), F32),
        ],
        flops=7e8,
        moved=8e6,
        mib=20,
    )(logit_scale, over_x, over_x_other, text_own, text_other, pairs)
    by_plane = [[(d * n_plane + p) * 2 for p in range(n_plane)] for d in range(n_dp)]
    by_dp = [[(d * n_plane + p) * 2 + 1 for d in range(n_dp)] for p in range(n_plane)]
    got_totals = lax.all_to_all(
        totals_send,
        DP + CLIP,
        split_axis=0,
        concat_axis=0,
        tiled=True,
        axis_index_groups=by_plane + by_dp,
    )
    (totals,) = local(totals_body, [((8, group_rows), F32)], 0, 1)(got_totals)
    totals_other = lax.ppermute(totals, "core", SWAP)

    video_part, text_part = local(
        functools.partial(grad_body, n_loc, n_clip),
        [((half, joint), BF16), ((n_lane, joint), BF16)],
        1,
        7,
        scratch=[pltpu.VMEM((group_rows, 2 * n_lane), BF16)],
        flops=2e8,
    )(logit_scale, expo, totals, totals_other, pairs, text_own, text_other, video_b)

    got_video = exchange(video_part.reshape(n_plane, n_loc, joint), PLANE)
    d_send, d_own = local(
        projected_body, [((n_plane, n_loc, joint), BF16), ((n_loc, joint), BF16)], 0, 3
    )(got_video, unit_own, norm_own)
    d_half, d_own = lax.optimization_barrier((exchange(d_send, PLANE).reshape(half, joint), d_own))
    d_half_other = lax.ppermute(d_half, "core", SWAP)

    summary_cols = lax.dynamic_slice(summaries, (0, lane_id * w_rows), (group_rows, w_rows))
    summary_cols = jnp.pad(summary_cols, ((0, 0), (0, w_pad - w_rows)))
    d_half, summary_cols = lax.optimization_barrier((d_half, summary_cols))
    piece = w_pad // n_z
    spare = -(-piece // 8) * 8
    (parts,) = local(weight_body, [((n_z, 2 * n_loc + spare, joint), BF16)], 0, 4, flops=3e7)(
        summary_cols, d_half, d_half_other, text_part
    )
    got_z, d_own = lax.optimization_barrier((exchange(parts, "z"), d_own))
    here, away = local(
        z_sum_body, [((n_loc + spare, joint), F32), ((n_loc + spare, joint), BF16)], 0, 1
    )(got_z)
    got_yh = lax.ppermute(away, "yh", SWAP)

    (d_clips,) = local(
        clips_body,
        [((n_loc, n_clips, width), BF16)],
        0,
        1,
        4,
        scratch=stage + [pltpu.VMEM((width, joint), BF16), pltpu.SemaphoreType.DMA((4,))],
        flops=2e7,
        moved=3e6,
    )(d_own, pool_query, clip_counts, clip_embed, full_weight)
    piece_send, d_text = local(
        functools.partial(yh_sum_body, n_loc),
        [((n_z, spare, joint), F32), ((n_loc, joint), F32)],
        0,
        2,
    )(here, got_yh)
    piece_send, d_clips = lax.optimization_barrier((piece_send, d_clips))
    d_weight, d_texts = local(
        functools.partial(last_body, piece), [((w_rows, joint), F32), ((n_loc, joint), F32)], 0, 3
    )(exchange(piece_send, "z"), d_text, text_embed)
    return (d_clips, d_weight, d_texts)


def solution(mesh):
    fine = Mesh(mesh.devices.reshape(2, 8, 4, 4, 2), DP + CLIP)
    everywhere = DP + CLIP
    return jax.shard_map(
        shards,
        mesh=fine,
        in_specs=(
            P(everywhere, None, None),
            P(everywhere),
            P(),
            P(CLIP, None),
            P(everywhere, None),
            P(),
            P(),
        ),
        out_specs=(P(everywhere, None, None), P(CLIP, None), P(everywhere, None)),
        check_vma=False,
    )
```

```python
import functools

import jax
import jax.numpy as jnp
from jax import lax
from jax.experimental import pallas as pl
from jax.experimental.pallas import tpu as pltpu
from jax.sharding import Mesh, PartitionSpec as P

EPS = 1e-06
F32 = jnp.float32
BF16 = jnp.bfloat16
DP = ("yh", "z")
CLIP = ("yl", "x", "core")
PLANE = ("yl", "x")
SWAP = [(0, 1), (1, 0)]


def unit_rows(values):
    norm_value = jnp.sqrt(jnp.sum(values * values, axis=1, keepdims=True) + EPS)
    return (values / norm_value, norm_value)


def exchange(blocks, axes):
    return lax.all_to_all(blocks, axes, split_axis=0, concat_axis=0, tiled=True)


def dot(a, b, contract):
    return lax.dot_general(a, b, (contract, ((), ())), preferred_element_type=F32)


def local(body, outs, n_scalars, n_args, n_far=0, scratch=(), flops=1e6, moved=1e6, mib=8):
    vmem = pl.BlockSpec(memory_space=pltpu.VMEM)
    smem = pl.BlockSpec(memory_space=pltpu.SMEM)
    far = pl.BlockSpec(memory_space=pltpu.HBM)
    return pl.pallas_call(
        body,
        out_shape=tuple(jax.ShapeDtypeStruct(shape, dtype) for shape, dtype in outs),
        in_specs=[smem] * n_scalars + [vmem] * n_args + [far] * n_far,
        out_specs=tuple(vmem for _ in outs),
        scratch_shapes=list(scratch),
        compiler_params=pltpu.CompilerParams(vmem_limit_bytes=mib * 1024 * 1024),
        cost_estimate=pl.CostEstimate(flops=int(flops), bytes_accessed=int(moved), transcendentals=0),
    )


def pool(counts_ref, embed, query):
    n_loc, n_clips, _ = embed.shape
    scores = jnp.sum(embed * query[None], axis=2, keepdims=True)
    video = lax.broadcasted_iota(jnp.int32, (n_loc, n_clips, 1), 0)
    clip = lax.broadcasted_iota(jnp.int32, (n_loc, n_clips, 1), 1)
    count = jnp.zeros((n_loc, n_clips, 1), jnp.int32)
    for v in range(n_loc):
        count = jnp.where(video == v, counts_ref[v], count)
    usable = clip < count
    masked = jnp.where(usable, scores, -1e30)
    raised = jnp.where(usable, jnp.exp(masked - jnp.max(masked, axis=1, keepdims=True)), 0.0)
    weights = raised / jnp.sum(raised, axis=1, keepdims=True)
    return weights, jnp.sum(weights * embed, axis=1)


def fetch(sources, targets, sems):
    copies = [
        pltpu.make_async_copy(source, target, sems.at[i])
        for i, (source, target) in enumerate(zip(sources, targets))
    ]
    for copy in copies:
        copy.start()
    for copy in copies:
        copy.wait()


def pool_body(
    query_hbm, counts_hbm, clips_hbm, rows_hbm, text_hbm, payload_ref, send_ref,
    query_ref, counts_ref, clips_ref, rows_ref, text_ref, sems,
):
    fetch(
        (query_hbm, counts_hbm, clips_hbm, rows_hbm, text_hbm),
        (query_ref, counts_ref, clips_ref, rows_ref, text_ref),
        sems,
    )
    unit, _ = unit_rows(text_ref[...].astype(F32))
    send_ref[...] = jnp.broadcast_to(unit[None], send_ref.shape).astype(BF16)
    n_loc, _, width = clips_ref.shape
    w_rows, joint = rows_ref.shape
    w_pad = payload_ref.shape[0] - 2 * n_loc
    _, summary = pool(counts_ref, clips_ref[...].astype(F32), query_ref[...].astype(F32).reshape(1, width))
    high = jnp.concatenate(
        [summary[:, joint:], jnp.zeros((n_loc, 2 * joint - width), F32)], axis=1
    )
    tail = jnp.zeros((w_pad - w_rows, joint), F32)
    payload_ref[...] = jnp.concatenate(
        [rows_ref[...].astype(F32), tail, summary[:, :joint], high], axis=0
    ).astype(BF16)


def clips_body(
    d_own_ref, query_hbm, counts_hbm, clips_hbm, weight_hbm, out_ref,
    query_ref, counts_ref, clips_ref, weight_ref, sems,
):
    fetch(
        (query_hbm, counts_hbm, clips_hbm, weight_hbm),
        (query_ref, counts_ref, clips_ref, weight_ref),
        sems,
    )
    embed = clips_ref[...].astype(F32)
    query = query_ref[...].astype(F32).reshape(1, embed.shape[2])
    weights, summary = pool(counts_ref, embed, query)
    d_summary = dot(d_own_ref[...], weight_ref[...], ((1,), (1,)))
    aligned = jnp.sum(embed * d_summary[:, None, :], axis=2, keepdims=True)
    baseline = jnp.sum(d_summary * summary, axis=1, keepdims=True)
    d_scores = weights * (aligned - baseline[:, None, :])
    out_ref[...] = (weights * d_summary[:, None, :] + d_scores * query[None]).astype(BF16)


def column(row):
    return jnp.broadcast_to(row, (128, row.shape[1])).T[:, :1]


def logits_body(
    n_loc, w_rows, scale_ref, own_ref, other_ref, text_own_ref, text_other_ref,
    _, weight_ref, summary_ref, video_ref, unit_ref, norm_ref, expo_ref, send_ref,
    weight_f, summary_f, unit_f, norm_f,
):
    n_x, n_yl, _, joint = own_ref.shape
    width = weight_ref.shape[0]
    half = n_x * n_yl * n_loc
    w_pad = -(-w_rows // 16) * 16
    first = lax.axis_index("core") == 0
    yl_id = lax.axis_index("yl")
    for x in range(n_x):
        for yl in range(n_yl):
            slot = jnp.bitwise_xor(yl_id, yl)
            own = own_ref[x, slot].astype(F32)
            other = other_ref[x, slot].astype(F32)
            pair = (jnp.where(first, own, other), jnp.where(first, other, own))
            for core in range(2):
                at = ((yl * n_x + x) * 2 + core) * w_rows
                weight_f[at : at + w_rows, :] = pair[core][:w_rows]
                row = core * half + (yl * n_x + x) * n_loc
                summary_f[row : row + n_loc, :joint] = pair[core][w_pad : w_pad + n_loc]
                summary_f[row : row + n_loc, joint:] = pair[core][w_pad + n_loc :, : width - joint]
    weight_b = weight_f[...].astype(BF16)
    summary_b = summary_f[...].astype(BF16)
    weight_ref[...] = weight_b
    summary_ref[...] = summary_b
    unit, norm = unit_rows(dot(summary_b, weight_b, ((1,), (0,))))
    video_b = unit.astype(BF16)
    video_ref[...] = video_b
    unit_f[...] = unit
    norm_f[...] = jnp.broadcast_to(norm, norm_f.shape)
    place = (lax.axis_index("core") * n_yl + yl_id) * n_x + lax.axis_index("x")
    mine = pl.ds(pl.multiple_of(place * n_loc, n_loc), n_loc)
    unit_ref[...] = unit_f[mine, :]
    norm_ref[...] = norm_f[mine, :]
    n_lane = text_own_ref.shape[0]
    scale = scale_ref[0]
    expo_ref[:, :n_lane] = jnp.exp(scale * dot(video_b, text_own_ref[...], ((1,), (1,))))
    expo_ref[:, n_lane:] = jnp.exp(scale * dot(video_b, text_other_ref[...], ((1,), (1,))))
    expo = expo_ref[...]
    row_part = jnp.broadcast_to(jnp.sum(expo, axis=1, keepdims=True), (2 * half, 128)).T[:1]
    col_part = jnp.sum(expo, axis=0, keepdims=True)
    send_ref[...] = jnp.broadcast_to(jnp.where(first, row_part, col_part)[None], send_ref.shape)


def totals_body(got_ref, out_ref):
    out_ref[...] = jnp.broadcast_to(jnp.sum(got_ref[...], axis=0), out_ref.shape)


def grad_body(
    n_loc, n_clip, scale_ref, expo_ref, totals_ref, totals_other_ref, pairs_ref, text_own_ref,
    text_other_ref, video_ref, part_ref, text_part_ref, grad_ref,
):
    n_lane = text_own_ref.shape[0]
    own = totals_ref[:1]
    other = totals_other_ref[:1]
    first = lax.axis_index("core") == 0
    swapped = jnp.concatenate([other[:, n_lane:], other[:, :n_lane]], axis=1)
    rows = jnp.where(first, own, other)
    cols = jnp.where(first, swapped, own)
    core = lax.axis_index("core")
    plane = lax.axis_index("yl") * lax.axis_size("x") + lax.axis_index("x")
    at = lax.broadcasted_iota(jnp.int32, (1, 2 * n_lane), 1)
    lane = jnp.where(at < n_lane, plane * 2 + core, plane * 2 + (1 - core))
    slot = jnp.where(at < n_lane, at, at - n_lane)
    col_id = ((slot // n_loc) * n_clip + lane) * n_loc + slot % n_loc
    group = lax.axis_index("yh") * lax.axis_size("z") + lax.axis_index("z")
    pairs = column(pairs_ref[pl.ds(group, 1), :].astype(F32)).astype(jnp.int32)
    pairs = pairs.reshape(-1, 2, n_loc, 1)
    pairs = jnp.concatenate([pairs[:, 0], pairs[:, 1]], axis=0).reshape(-1, 1)
    positive = jnp.where(pairs == col_id, 1.0, 0.0)
    expo = expo_ref[...]
    grad = (expo / column(rows) + expo / cols) * 0.5 - positive
    grad_ref[...] = grad.astype(BF16)
    half = expo.shape[0] // 2
    mine = grad_ref[pl.ds(pl.multiple_of(core * half, half), half), :]
    part = dot(mine[:, :n_lane], text_own_ref[...], ((1,), (0,)))
    part = part + dot(mine[:, n_lane:], text_other_ref[...], ((1,), (0,)))
    part_ref[...] = (scale_ref[0] * part).astype(BF16)
    text_part = dot(grad_ref[:, :n_lane], video_ref[...], ((0,), (0,)))
    text_part_ref[...] = (scale_ref[0] * text_part).astype(BF16)


def projected_body(part_ref, unit_ref, norm_ref, out_ref, own_ref):
    d_video = jnp.sum(part_ref[...].astype(F32), axis=0)
    unit = unit_ref[...]
    norm = norm_ref[:, :1]
    value = (d_video - unit * jnp.sum(unit * d_video, axis=1, keepdims=True)) / norm
    out_ref[...] = jnp.broadcast_to(value[None], out_ref.shape).astype(BF16)
    own_ref[...] = value.astype(BF16)


def weight_body(cols_ref, own_ref, other_ref, text_ref, out_ref):
    n_z, _, joint = out_ref.shape
    half = own_ref.shape[0]
    core = lax.axis_index("core")
    yh_id = lax.axis_index("yh")
    own_cols = cols_ref[pl.ds(pl.multiple_of(core * half, half), half), :]
    other_cols = cols_ref[pl.ds(pl.multiple_of((1 - core) * half, half), half), :]
    part = dot(own_cols, own_ref[...], ((0,), (0,))) + dot(other_cols, other_ref[...], ((0,), (0,)))
    n_text = text_ref.shape[0] // 2
    n_loc = n_text // n_z
    piece = part.shape[0] // n_z
    spare = out_ref.shape[1] - 2 * n_loc - piece
    here = text_ref[pl.ds(pl.multiple_of(yh_id * n_text, n_text), n_text), :].astype(F32)
    away = text_ref[pl.ds(pl.multiple_of((1 - yh_id) * n_text, n_text), n_text), :].astype(F32)
    for z in range(n_z):
        rows = jnp.concatenate(
            [
                here[z * n_loc : (z + 1) * n_loc],
                away[z * n_loc : (z + 1) * n_loc],
                part[z * piece : (z + 1) * piece],
                jnp.zeros((spare, joint), F32),
            ],
            axis=0,
        )
        out_ref[z] = rows.astype(BF16)


def z_sum_body(got_ref, here_ref, away_ref):
    total = jnp.sum(got_ref[...].astype(F32), axis=0)
    n_loc = here_ref.shape[0] // 2
    piece = total[2 * n_loc :]
    here_ref[...] = jnp.concatenate([total[:n_loc], piece], axis=0)
    away_ref[...] = jnp.concatenate([total[n_loc : 2 * n_loc], piece], axis=0).astype(BF16)


def yh_sum_body(n_loc, here_ref, got_ref, out_ref, text_ref):
    total = here_ref[...] + got_ref[...].astype(F32)
    text_ref[...] = total[:n_loc]
    out_ref[...] = jnp.broadcast_to(total[None, n_loc:], out_ref.shape).astype(BF16)


def last_body(piece, got_ref, d_text_ref, text_ref, out_ref, d_texts_ref):
    rows = [got_ref[z].astype(F32)[:piece] for z in range(got_ref.shape[0])]
    out_ref[...] = jnp.concatenate(rows, axis=0)[: out_ref.shape[0]]
    unit, norm = unit_rows(text_ref[...].astype(F32))
    d_text = d_text_ref[...]
    d_texts_ref[...] = (d_text - unit * jnp.sum(unit * d_text, axis=1, keepdims=True)) / norm


def shards(clip_embed, clip_counts, pool_query, proj_weight, text_embed, pair_index, logit_scale):
    n_loc, n_clips, width = clip_embed.shape
    w_rows, joint = proj_weight.shape
    n_dp, n_yh, n_z = lax.axis_size(DP), lax.axis_size("yh"), lax.axis_size("z")
    n_yl, n_x, n_clip = lax.axis_size("yl"), lax.axis_size("x"), lax.axis_size(CLIP)
    n_plane = n_yl * n_x
    group_rows = n_loc * n_clip
    half = group_rows // 2
    n_lane = n_dp * n_loc
    core_id = lax.axis_index("core")
    plane_id = lax.axis_index(PLANE)
    lane_id = lax.axis_index(CLIP)
    group_id = lax.axis_index(DP)
    w_pad = -(-w_rows // 16) * 16
    stage = [
        pltpu.VMEM((width,), BF16),
        pltpu.SMEM((n_loc,), jnp.int32),
        pltpu.VMEM((n_loc, n_clips, width), BF16),
    ]
    payload, text_send = local(
        pool_body,
        [((w_pad + 2 * n_loc, joint), BF16), ((n_dp, n_loc, joint), BF16)],
        0,
        0,
        5,
        scratch=stage
        + [
            pltpu.VMEM((w_rows, joint), BF16),
            pltpu.VMEM((n_loc, joint), BF16),
            pltpu.SemaphoreType.DMA((5,)),
        ],
        mib=56,
    )(pool_query, clip_counts, clip_embed, proj_weight, text_embed)
    text_own = exchange(text_send, DP).reshape(n_lane, joint)
    text_other = lax.ppermute(text_own, "core", SWAP)

    near = [payload] + [
        lax.ppermute(payload, "yl", [(i, i ^ k) for i in range(n_yl)]) for k in range(1, n_yl)
    ]
    over_y = jnp.stack(near)
    over_y, text_own, text_other = lax.optimization_barrier((over_y, text_own, text_other))
    over_x = exchange(jnp.broadcast_to(over_y[None], (n_x, *over_y.shape)), "x")

    pairs = pair_index.reshape(n_dp, group_rows)
    over_x_other = lax.ppermute(over_x, "core", SWAP)

    full_weight, summaries, video_b, unit_own, norm_own, expo, totals_send = local(
        functools.partial(logits_body, n_loc, w_rows),
        [
            ((width, joint), BF16),
            ((group_rows, width), BF16),
            ((group_rows, joint), BF16),
            ((n_loc, joint), F32),
            ((n_loc, 128), F32),
            ((group_rows, 2 * n_lane), F32),
            ((n_plane, 1, group_rows), F32),
        ],
        1,
        5,
        scratch=[
            pltpu.VMEM((width, joint), F32),
            pltpu.VMEM((group_rows, width), F32),
            pltpu.VMEM((group_rows, joint), F32),
            pltpu.VMEM((group_rows, 128), F32),
        ],
        flops=7e8,
        moved=8e6,
        mib=20,
    )(logit_scale, over_x, over_x_other, text_own, text_other, pairs)
    by_plane = [[(d * n_plane + p) * 2 for p in range(n_plane)] for d in range(n_dp)]
    by_dp = [[(d * n_plane + p) * 2 + 1 for d in range(n_dp)] for p in range(n_plane)]
    got_totals = lax.all_to_all(
        totals_send,
        DP + CLIP,
        split_axis=0,
        concat_axis=0,
        tiled=True,
        axis_index_groups=by_plane + by_dp,
    )
    (totals,) = local(totals_body, [((8, group_rows), F32)], 0, 1)(got_totals)
    totals_other = lax.ppermute(totals, "core", SWAP)

    video_part, text_part = local(
        functools.partial(grad_body, n_loc, n_clip),
        [((half, joint), BF16), ((n_lane, joint), BF16)],
        1,
        7,
        scratch=[pltpu.VMEM((group_rows, 2 * n_lane), BF16)],
        flops=2e8,
    )(logit_scale, expo, totals, totals_other, pairs, text_own, text_other, video_b)

    got_video = exchange(video_part.reshape(n_plane, n_loc, joint), PLANE)
    d_send, d_own = local(
        projected_body, [((n_plane, n_loc, joint), BF16), ((n_loc, joint), BF16)], 0, 3
    )(got_video, unit_own, norm_own)
    d_half, d_own = lax.optimization_barrier((exchange(d_send, PLANE).reshape(half, joint), d_own))
    d_half_other = lax.ppermute(d_half, "core", SWAP)

    summary_cols = lax.dynamic_slice(summaries, (0, lane_id * w_rows), (group_rows, w_rows))
    summary_cols = jnp.pad(summary_cols, ((0, 0), (0, w_pad - w_rows)))
    d_half, summary_cols = lax.optimization_barrier((d_half, summary_cols))
    piece = w_pad // n_z
    spare = -(-piece // 8) * 8
    (parts,) = local(weight_body, [((n_z, 2 * n_loc + spare, joint), BF16)], 0, 4, flops=3e7)(
        summary_cols, d_half, d_half_other, text_part
    )
    got_z, d_own = lax.optimization_barrier((exchange(parts, "z"), d_own))
    here, away = local(
        z_sum_body, [((n_loc + spare, joint), F32), ((n_loc + spare, joint), BF16)], 0, 1
    )(got_z)
    got_yh = lax.ppermute(away, "yh", SWAP)

    (d_clips,) = local(
        clips_body,
        [((n_loc, n_clips, width), BF16)],
        0,
        1,
        4,
        scratch=stage + [pltpu.VMEM((width, joint), BF16), pltpu.SemaphoreType.DMA((4,))],
        flops=2e7,
        moved=3e6,
    )(d_own, pool_query, clip_counts, clip_embed, full_weight)
    piece_send, d_text = local(
        functools.partial(yh_sum_body, n_loc),
        [((n_z, spare, joint), BF16), ((n_loc, joint), F32)],
        0,
        2,
    )(here, got_yh)
    piece_send, d_clips = lax.optimization_barrier((piece_send, d_clips))
    d_weight, d_texts = local(
        functools.partial(last_body, piece), [((w_rows, joint), F32), ((n_loc, joint), F32)], 0, 3
    )(exchange(piece_send, "z"), d_text, text_embed)
    return (d_clips, d_weight, d_texts)


def solution(mesh):
    fine = Mesh(mesh.devices.reshape(2, 8, 4, 4, 2), DP + CLIP)
    everywhere = DP + CLIP
    return jax.shard_map(
        shards,
        mesh=fine,
        in_specs=(
            P(everywhere, None, None),
            P(everywhere),
            P(),
            P(CLIP, None),
            P(everywhere, None),
            P(),
            P(),
        ),
        out_specs=(P(everywhere, None, None), P(CLIP, None), P(everywhere, None)),
        check_vma=False,
    )
```

```python
import functools

import jax
import jax.numpy as jnp
from jax import lax
from jax.experimental import pallas as pl
from jax.experimental.pallas import tpu as pltpu
from jax.sharding import Mesh, PartitionSpec as P

EPS = 1e-06
F32 = jnp.float32
BF16 = jnp.bfloat16
DP = ("yh", "z")
CLIP = ("yl", "x", "core")
PLANE = ("yl", "x")
SWAP = [(0, 1), (1, 0)]


def unit_rows(values):
    norm_value = jnp.sqrt(jnp.sum(values * values, axis=1, keepdims=True) + EPS)
    return (values / norm_value, norm_value)


def exchange(blocks, axes):
    return lax.all_to_all(blocks, axes, split_axis=0, concat_axis=0, tiled=True)


def dot(a, b, contract):
    return lax.dot_general(a, b, (contract, ((), ())), preferred_element_type=F32)


def local(body, outs, n_scalars, n_args, n_far=0, scratch=(), flops=1e6, moved=1e6, mib=8):
    vmem = pl.BlockSpec(memory_space=pltpu.VMEM)
    smem = pl.BlockSpec(memory_space=pltpu.SMEM)
    far = pl.BlockSpec(memory_space=pltpu.HBM)
    return pl.pallas_call(
        body,
        out_shape=tuple(jax.ShapeDtypeStruct(shape, dtype) for shape, dtype in outs),
        in_specs=[smem] * n_scalars + [vmem] * n_args + [far] * n_far,
        out_specs=tuple(vmem for _ in outs),
        scratch_shapes=list(scratch),
        compiler_params=pltpu.CompilerParams(vmem_limit_bytes=mib * 1024 * 1024),
        cost_estimate=pl.CostEstimate(flops=int(flops), bytes_accessed=int(moved), transcendentals=0),
    )


def pool(counts_ref, embed, query):
    n_loc, n_clips, _ = embed.shape
    scores = jnp.sum(embed * query[None], axis=2, keepdims=True)
    video = lax.broadcasted_iota(jnp.int32, (n_loc, n_clips, 1), 0)
    clip = lax.broadcasted_iota(jnp.int32, (n_loc, n_clips, 1), 1)
    count = jnp.zeros((n_loc, n_clips, 1), jnp.int32)
    for v in range(n_loc):
        count = jnp.where(video == v, counts_ref[v], count)
    usable = clip < count
    masked = jnp.where(usable, scores, -1e30)
    raised = jnp.where(usable, jnp.exp(masked - jnp.max(masked, axis=1, keepdims=True)), 0.0)
    weights = raised / jnp.sum(raised, axis=1, keepdims=True)
    return weights, jnp.sum(weights * embed, axis=1)


def fetch(sources, targets, sems):
    copies = [
        pltpu.make_async_copy(source, target, sems.at[i])
        for i, (source, target) in enumerate(zip(sources, targets))
    ]
    for copy in copies:
        copy.start()
    for copy in copies:
        copy.wait()


def pool_body(
    query_hbm, counts_hbm, clips_hbm, rows_hbm, text_hbm, payload_ref, send_ref,
    query_ref, counts_ref, clips_ref, rows_ref, text_ref, sems,
):
    fetch(
        (query_hbm, counts_hbm, clips_hbm, rows_hbm, text_hbm),
        (query_ref, counts_ref, clips_ref, rows_ref, text_ref),
        sems,
    )
    unit, _ = unit_rows(text_ref[...].astype(F32))
    send_ref[...] = jnp.broadcast_to(unit[None], send_ref.shape).astype(BF16)
    n_loc, _, width = clips_ref.shape
    w_rows, joint = rows_ref.shape
    w_pad = payload_ref.shape[0] - 2 * n_loc
    _, summary = pool(counts_ref, clips_ref[...].astype(F32), query_ref[...].astype(F32).reshape(1, width))
    high = jnp.concatenate(
        [summary[:, joint:], jnp.zeros((n_loc, 2 * joint - width), F32)], axis=1
    )
    tail = jnp.zeros((w_pad - w_rows, joint), F32)
    payload_ref[...] = jnp.concatenate(
        [rows_ref[...].astype(F32), tail, summary[:, :joint], high], axis=0
    ).astype(BF16)


def clips_body(
    d_own_ref, query_hbm, counts_hbm, clips_hbm, weight_hbm, out_ref,
    query_ref, counts_ref, clips_ref, weight_ref, sems,
):
    fetch(
        (query_hbm, counts_hbm, clips_hbm, weight_hbm),
        (query_ref, counts_ref, clips_ref, weight_ref),
        sems,
    )
    embed = clips_ref[...].astype(F32)
    query = query_ref[...].astype(F32).reshape(1, embed.shape[2])
    weights, summary = pool(counts_ref, embed, query)
    d_summary = dot(d_own_ref[...], weight_ref[...], ((1,), (1,)))
    aligned = jnp.sum(embed * d_summary[:, None, :], axis=2, keepdims=True)
    baseline = jnp.sum(d_summary * summary, axis=1, keepdims=True)
    d_scores = weights * (aligned - baseline[:, None, :])
    out_ref[...] = (weights * d_summary[:, None, :] + d_scores * query[None]).astype(BF16)


def column(row):
    return jnp.broadcast_to(row, (128, row.shape[1])).T[:, :1]


def logits_body(
    n_loc, w_rows, scale_ref, own_ref, other_ref, text_own_ref, text_other_ref,
    _, weight_ref, summary_ref, video_ref, unit_ref, norm_ref, expo_ref, send_ref,
    weight_f, summary_f, unit_f, norm_f,
):
    n_x, n_yl, _, joint = own_ref.shape
    width = weight_ref.shape[0]
    half = n_x * n_yl * n_loc
    w_pad = -(-w_rows // 16) * 16
    first = lax.axis_index("core") == 0
    yl_id = lax.axis_index("yl")
    for x in range(n_x):
        for yl in range(n_yl):
            slot = jnp.bitwise_xor(yl_id, yl)
            own = own_ref[x, slot].astype(F32)
            other = other_ref[x, slot].astype(F32)
            pair = (jnp.where(first, own, other), jnp.where(first, other, own))
            for core in range(2):
                at = ((yl * n_x + x) * 2 + core) * w_rows
                weight_f[at : at + w_rows, :] = pair[core][:w_rows]
                row = core * half + (yl * n_x + x) * n_loc
                summary_f[row : row + n_loc, :joint] = pair[core][w_pad : w_pad + n_loc]
                summary_f[row : row + n_loc, joint:] = pair[core][w_pad + n_loc :, : width - joint]
    weight_b = weight_f[...].astype(BF16)
    summary_b = summary_f[...].astype(BF16)
    weight_ref[...] = weight_b
    summary_ref[...] = summary_b
    unit, norm = unit_rows(dot(summary_b, weight_b, ((1,), (0,))))
    video_b = unit.astype(BF16)
    video_ref[...] = video_b
    unit_f[...] = unit
    norm_f[...] = jnp.broadcast_to(norm, norm_f.shape)
    place = (lax.axis_index("core") * n_yl + yl_id) * n_x + lax.axis_index("x")
    mine = pl.ds(pl.multiple_of(place * n_loc, n_loc), n_loc)
    unit_ref[...] = unit_f[mine, :]
    norm_ref[...] = norm_f[mine, :]
    n_lane = text_own_ref.shape[0]
    scale = scale_ref[0]
    expo_ref[:, :n_lane] = jnp.exp(scale * dot(video_b, text_own_ref[...], ((1,), (1,))))
    expo_ref[:, n_lane:] = jnp.exp(scale * dot(video_b, text_other_ref[...], ((1,), (1,))))
    expo = expo_ref[...]
    row_part = jnp.broadcast_to(jnp.sum(expo, axis=1, keepdims=True), (2 * half, 128)).T[:1]
    col_part = jnp.sum(expo, axis=0, keepdims=True)
    send_ref[...] = jnp.broadcast_to(jnp.where(first, row_part, col_part)[None], send_ref.shape)


def totals_body(got_ref, out_ref):
    out_ref[...] = jnp.broadcast_to(jnp.sum(got_ref[...], axis=0), out_ref.shape)


def grad_body(
    n_loc, n_clip, scale_ref, expo_ref, totals_ref, totals_other_ref, pairs_ref, text_own_ref,
    text_other_ref, video_ref, part_ref, text_part_ref, grad_ref,
):
    n_lane = text_own_ref.shape[0]
    own = totals_ref[:1]
    other = totals_other_ref[:1]
    first = lax.axis_index("core") == 0
    swapped = jnp.concatenate([other[:, n_lane:], other[:, :n_lane]], axis=1)
    rows = jnp.where(first, own, other)
    cols = jnp.where(first, swapped, own)
    core = lax.axis_index("core")
    plane = lax.axis_index("yl") * lax.axis_size("x") + lax.axis_index("x")
    at = lax.broadcasted_iota(jnp.int32, (1, 2 * n_lane), 1)
    lane = jnp.where(at < n_lane, plane * 2 + core, plane * 2 + (1 - core))
    slot = jnp.where(at < n_lane, at, at - n_lane)
    col_id = ((slot // n_loc) * n_clip + lane) * n_loc + slot % n_loc
    group = lax.axis_index("yh") * lax.axis_size("z") + lax.axis_index("z")
    pairs = column(pairs_ref[pl.ds(group, 1), :].astype(F32)).astype(jnp.int32)
    pairs = pairs.reshape(-1, 2, n_loc, 1)
    pairs = jnp.concatenate([pairs[:, 0], pairs[:, 1]], axis=0).reshape(-1, 1)
    positive = jnp.where(pairs == col_id, 1.0, 0.0)
    expo = expo_ref[...]
    grad = (expo / column(rows) + expo / cols) * 0.5 - positive
    grad_ref[...] = grad.astype(BF16)
    half = expo.shape[0] // 2
    mine = grad_ref[pl.ds(pl.multiple_of(core * half, half), half), :]
    part = dot(mine[:, :n_lane], text_own_ref[...], ((1,), (0,)))
    part = part + dot(mine[:, n_lane:], text_other_ref[...], ((1,), (0,)))
    part_ref[...] = (scale_ref[0] * part).astype(BF16)
    text_part = dot(grad_ref[:, :n_lane], video_ref[...], ((0,), (0,)))
    text_part_ref[...] = (scale_ref[0] * text_part).astype(BF16)


def projected_body(part_ref, unit_ref, norm_ref, out_ref, own_ref):
    d_video = jnp.sum(part_ref[...].astype(F32), axis=0)
    unit = unit_ref[...]
    norm = norm_ref[:, :1]
    value = (d_video - unit * jnp.sum(unit * d_video, axis=1, keepdims=True)) / norm
    out_ref[...] = jnp.broadcast_to(value[None], out_ref.shape).astype(BF16)
    own_ref[...] = value.astype(BF16)


def weight_body(cols_ref, own_ref, other_ref, text_ref, out_ref):
    n_z, _, joint = out_ref.shape
    half = own_ref.shape[0]
    core = lax.axis_index("core")
    yh_id = lax.axis_index("yh")
    own_cols = cols_ref[pl.ds(pl.multiple_of(core * half, half), half), :]
    other_cols = cols_ref[pl.ds(pl.multiple_of((1 - core) * half, half), half), :]
    part = dot(own_cols, own_ref[...], ((0,), (0,))) + dot(other_cols, other_ref[...], ((0,), (0,)))
    n_text = text_ref.shape[0] // 2
    n_loc = n_text // n_z
    piece = part.shape[0] // n_z
    spare = out_ref.shape[1] - 2 * n_loc - piece
    here = text_ref[pl.ds(pl.multiple_of(yh_id * n_text, n_text), n_text), :].astype(F32)
    away = text_ref[pl.ds(pl.multiple_of((1 - yh_id) * n_text, n_text), n_text), :].astype(F32)
    for z in range(n_z):
        rows = jnp.concatenate(
            [
                here[z * n_loc : (z + 1) * n_loc],
                away[z * n_loc : (z + 1) * n_loc],
                part[z * piece : (z + 1) * piece],
                jnp.zeros((spare, joint), F32),
            ],
            axis=0,
        )
        out_ref[z] = rows.astype(BF16)


def z_sum_body(got_ref, here_ref, away_ref):
    total = jnp.sum(got_ref[...].astype(F32), axis=0)
    n_loc = here_ref.shape[0] // 2
    piece = total[2 * n_loc :]
    here_ref[...] = jnp.concatenate([total[:n_loc], piece], axis=0)
    away_ref[...] = jnp.concatenate([total[n_loc : 2 * n_loc], piece], axis=0).astype(BF16)


def yh_sum_body(n_loc, here_ref, got_ref, out_ref, text_ref):
    total = here_ref[...] + got_ref[...].astype(F32)
    text_ref[...] = total[:n_loc]
    out_ref[...] = jnp.broadcast_to(total[None, n_loc:], out_ref.shape).astype(BF16)


def last_body(piece, got_ref, d_text_ref, text_ref, out_ref, d_texts_ref):
    rows = [got_ref[z].astype(F32)[:piece] for z in range(got_ref.shape[0])]
    out_ref[...] = jnp.concatenate(rows, axis=0)[: out_ref.shape[0]]
    unit, norm = unit_rows(text_ref[...].astype(F32))
    d_text = d_text_ref[...]
    d_texts_ref[...] = (d_text - unit * jnp.sum(unit * d_text, axis=1, keepdims=True)) / norm


def shards(clip_embed, clip_counts, pool_query, proj_weight, text_embed, pair_index, logit_scale):
    n_loc, n_clips, width = clip_embed.shape
    w_rows, joint = proj_weight.shape
    n_dp, n_yh, n_z = lax.axis_size(DP), lax.axis_size("yh"), lax.axis_size("z")
    n_yl, n_x, n_clip = lax.axis_size("yl"), lax.axis_size("x"), lax.axis_size(CLIP)
    n_plane = n_yl * n_x
    group_rows = n_loc * n_clip
    half = group_rows // 2
    n_lane = n_dp * n_loc
    core_id = lax.axis_index("core")
    plane_id = lax.axis_index(PLANE)
    lane_id = lax.axis_index(CLIP)
    group_id = lax.axis_index(DP)
    w_pad = -(-w_rows // 16) * 16
    stage = [
        pltpu.VMEM((width,), BF16),
        pltpu.SMEM((n_loc,), jnp.int32),
        pltpu.VMEM((n_loc, n_clips, width), BF16),
    ]
    payload, text_send = local(
        pool_body,
        [((w_pad + 2 * n_loc, joint), BF16), ((n_dp, n_loc, joint), BF16)],
        0,
        0,
        5,
        scratch=stage
        + [
            pltpu.VMEM((w_rows, joint), BF16),
            pltpu.VMEM((n_loc, joint), BF16),
            pltpu.SemaphoreType.DMA((5,)),
        ],
        mib=56,
    )(pool_query, clip_counts, clip_embed, proj_weight, text_embed)
    text_own = exchange(text_send, DP).reshape(n_lane, joint)
    text_other = lax.ppermute(text_own, "core", SWAP)

    near = {0: payload}
    for k in range(n_yl - 1, 0, -1):
        near[k] = lax.ppermute(payload, "yl", [(i, i ^ k) for i in range(n_yl)])
    over_y = jnp.stack([near[k] for k in range(n_yl)])
    over_y, text_own = lax.optimization_barrier((over_y, text_own))
    over_x = exchange(jnp.broadcast_to(over_y[None], (n_x, *over_y.shape)), "x")

    pairs = pair_index.reshape(n_dp, group_rows)
    over_x_other = lax.ppermute(over_x, "core", SWAP)

    full_weight, summaries, video_b, unit_own, norm_own, expo, totals_send = local(
        functools.partial(logits_body, n_loc, w_rows),
        [
            ((width, joint), BF16),
            ((group_rows, width), BF16),
            ((group_rows, joint), BF16),
            ((n_loc, joint), F32),
            ((n_loc, 128), F32),
            ((group_rows, 2 * n_lane), F32),
            ((n_plane, 1, group_rows), F32),
        ],
        1,
        5,
        scratch=[
            pltpu.VMEM((width, joint), F32),
            pltpu.VMEM((group_rows, width), F32),
            pltpu.VMEM((group_rows, joint), F32),
            pltpu.VMEM((group_rows, 128), F32),
        ],
        flops=7e8,
        moved=8e6,
        mib=20,
    )(logit_scale, over_x, over_x_other, text_own, text_other, pairs)
    by_plane = [[(d * n_plane + p) * 2 for p in range(n_plane)] for d in range(n_dp)]
    by_dp = [[(d * n_plane + p) * 2 + 1 for d in range(n_dp)] for p in range(n_plane)]
    got_totals = lax.all_to_all(
        totals_send,
        DP + CLIP,
        split_axis=0,
        concat_axis=0,
        tiled=True,
        axis_index_groups=by_plane + by_dp,
    )
    (totals,) = local(totals_body, [((8, group_rows), F32)], 0, 1)(got_totals)
    totals_other = lax.ppermute(totals, "core", SWAP)

    video_part, text_part = local(
        functools.partial(grad_body, n_loc, n_clip),
        [((half, joint), BF16), ((n_lane, joint), BF16)],
        1,
        7,
        scratch=[pltpu.VMEM((group_rows, 2 * n_lane), BF16)],
        flops=2e8,
    )(logit_scale, expo, totals, totals_other, pairs, text_own, text_other, video_b)

    got_video = exchange(video_part.reshape(n_plane, n_loc, joint), PLANE)
    d_send, d_own = local(
        projected_body, [((n_plane, n_loc, joint), BF16), ((n_loc, joint), BF16)], 0, 3
    )(got_video, unit_own, norm_own)
    d_half, d_own = lax.optimization_barrier((exchange(d_send, PLANE).reshape(half, joint), d_own))
    d_half_other = lax.ppermute(d_half, "core", SWAP)

    summary_cols = lax.dynamic_slice(summaries, (0, lane_id * w_rows), (group_rows, w_rows))
    summary_cols = jnp.pad(summary_cols, ((0, 0), (0, w_pad - w_rows)))
    d_half, summary_cols = lax.optimization_barrier((d_half, summary_cols))
    piece = w_pad // n_z
    spare = -(-piece // 8) * 8
    (parts,) = local(weight_body, [((n_z, 2 * n_loc + spare, joint), BF16)], 0, 4, flops=3e7)(
        summary_cols, d_half, d_half_other, text_part
    )
    got_z, d_own = lax.optimization_barrier((exchange(parts, "z"), d_own))
    here, away = local(
        z_sum_body, [((n_loc + spare, joint), F32), ((n_loc + spare, joint), BF16)], 0, 1
    )(got_z)
    got_yh = lax.ppermute(away, "yh", SWAP)

    (d_clips,) = local(
        clips_body,
        [((n_loc, n_clips, width), BF16)],
        0,
        1,
        4,
        scratch=stage + [pltpu.VMEM((width, joint), BF16), pltpu.SemaphoreType.DMA((4,))],
        flops=2e7,
        moved=3e6,
    )(d_own, pool_query, clip_counts, clip_embed, full_weight)
    piece_send, d_text = local(
        functools.partial(yh_sum_body, n_loc),
        [((n_z, spare, joint), BF16), ((n_loc, joint), F32)],
        0,
        2,
    )(here, got_yh)
    piece_send, d_clips = lax.optimization_barrier((piece_send, d_clips))
    d_weight, d_texts = local(
        functools.partial(last_body, piece), [((w_rows, joint), F32), ((n_loc, joint), F32)], 0, 3
    )(exchange(piece_send, "z"), d_text, text_embed)
    return (d_clips, d_weight, d_texts)


def solution(mesh):
    fine = Mesh(mesh.devices.reshape(2, 8, 4, 4, 2), DP + CLIP)
    everywhere = DP + CLIP
    return jax.shard_map(
        shards,
        mesh=fine,
        in_specs=(
            P(everywhere, None, None),
            P(everywhere),
            P(),
            P(CLIP, None),
            P(everywhere, None),
            P(),
            P(),
        ),
        out_specs=(P(everywhere, None, None), P(CLIP, None), P(everywhere, None)),
        check_vma=False,
    )
```
